32 devices in a mesh: groups: 2 (over y), ops: 4 (over z), sec: 2 (over x), rep: 2 (over core).
Axes of the slice: x: 2, y: 2, z: 4, core: 2. Of those that a mesh axis runs over, the one named last changes fastest.
Arguments:
- correction: float32 [3, 64, 128, 128], P(None, ('groups', 'sec', 'rep'), 'ops'), parts along dimension 1, may hold values from -80 to 80
- left_blocks: float32 [1280, 128, 128], P(('groups', 'ops', 'sec', 'rep')), parts along dimension 0, may hold values from -0.5 to 0.5
- right_blocks: float32 [32, 128, 128], P(('groups', 'ops')), parts along dimension 0, may hold values from -0.125 to 0.125
- send_sector: int32 [8, 4, 2], P(('groups', 'sec', 'rep')), parts along dimension 0, may hold values from -1 to 7, as said below
- pair_slot: int32 [1280], P(('groups', 'ops', 'sec', 'rep')), parts along dimension 0, may hold values from 0 to 7, as said below
- pair_term: int32 [1280], P(('groups', 'ops', 'sec', 'rep')), parts along dimension 0, may hold values from 0 to 3
- pair_dst: int32 [1280], P(('groups', 'ops', 'sec', 'rep')), parts along dimension 0, may hold values from 0 to 7
- pair_live: int32 [1280], P(('groups', 'ops', 'sec', 'rep')), parts along dimension 0, may hold values from 0 to 1, as said below
Outputs:
- search_basis: float32 [3, 64, 128, 128], P(None, ('groups', 'sec', 'rep'), 'ops'), parts along dimension 1
- sigma_blocks: float32 [3, 64, 128, 128], P(None, ('groups', 'sec', 'rep'), 'ops'), parts along dimension 1
The draws below stay inside these ranges and needn't reach their ends.
There are 2 independent parts, one for each index of `groups`. The reference program is written for one: setup_inputs(seed, part) draws one part's arguments, and reference() takes and returns one part's arrays. A program takes and returns all parts, laid end to end along the dimension named above; each array names one. Nothing has to cross between parts.
Inputs may be any that keep to these rules, and one draw needn't show every extreme that they name: `send_sector`: slot 0 of every sender and receiver holds a sector; the two sectors of one sender and receiver differ; -1 marks an empty slot; some receiver gets 2 filled slots from every sender. `pair_slot`: every pair names a filled slot of its own holder's received slots, slot e * 2 + c being slot c from sender e. `pair_live`: the share of live pairs differs from device to device; some device has all 40 pairs live.
All inputs are finite; a program needn't handle non-finite values.
Results may differ from the reference program's by a relative error of at most 0.0003.
Values sent between devices are 32-bit elements; how exact they have to be, the bound alone decides.
No kernel may reach another device: no remote copies, remote signals or barrier semaphores. Data moves between devices by JAX's collectives and lax.ppermute only.
A program may use at most 64 MiB of HBM per device.

```python
import math
import jax
import jax.numpy as jnp
from jax import lax

BLK = 128
VECS = 3
CAP = 2
S_LOC = 8
K_DEV = 4
P_DEV = 40
S = 32
K = 16
PAIRS = 640
N_OPS = 4
N_SEC = 2
N_REP = 2


def route_counts(key):
    holders = N_SEC * N_REP
    key_one, key_two = jax.random.split(jax.random.fold_in(key, 101))
    counts = jax.random.randint(key_one, (holders, holders), 1, CAP + 1)
    favored = jax.random.randint(key_two, (), 0, holders)
    return jnp.where(jnp.arange(holders)[None, :] == favored, CAP, counts)


def draw_send_sector(key, part):
    counts = route_counts(key)
    key = jax.random.fold_in(key, 3)
    holders = N_SEC * N_REP
    key_one, key_two = jax.random.split(key)
    leading = jax.random.randint(key_one, (holders, holders), 0, S_LOC)
    offset = jax.random.randint(key_two, (holders, holders), 1, S_LOC)
    trailing = jnp.where(counts >= 2, (leading + offset) % S_LOC, -1)
    return jnp.stack([leading, trailing], axis=-1).astype(jnp.int32)


def draw_pair_slot(key, part):
    counts = route_counts(key)
    key = jax.random.fold_in(key, 5)
    holders = N_SEC * N_REP
    pairs = P_DEV * N_OPS * holders
    holder = jnp.arange(pairs) // P_DEV % holders
    key_one, key_two = jax.random.split(key)
    sender = jax.random.randint(key_one, (pairs,), 0, holders)
    chosen = jax.random.randint(key_two, (pairs,), 0, counts[sender, holder])
    return (sender * CAP + chosen).astype(jnp.int32)


def draw_pair_live(key, part):
    key = jax.random.fold_in(key, 11)
    holders = N_SEC * N_REP
    devices = N_OPS * holders
    key_one, key_two, key_three = jax.random.split(key, 3)
    levels = jax.random.randint(key_one, (devices,), 1, 5)
    favored = jax.random.randint(key_two, (), 0, devices)
    levels = jnp.where(jnp.arange(devices) == favored, 4, levels)
    rolled = jax.random.randint(key_three, (devices * P_DEV,), 0, 4)
    return (rolled < jnp.repeat(levels, P_DEV)).astype(jnp.int32)


def draw_correction(key, part):
    key = jax.random.fold_in(key, 7)
    key_one = jax.random.fold_in(key, 0)
    values = jax.random.normal(key_one, (VECS, S, BLK, BLK), jnp.float32)
    sector_ramp = jnp.exp(math.log(3.0) * jnp.arange(S, dtype=jnp.float32) / max(S - 1, 1))
    row_ramp = jnp.exp(math.log(3.0) * jnp.arange(BLK, dtype=jnp.float32) / (BLK - 1))
    values = values * sector_ramp[None, :, None, None] * row_ramp[None, None, :, None]
    return jnp.clip(values, -80.0, 80.0).astype(jnp.float32)


def touch_ends(result, own_key, smallest, top_value):
    index_at = [jax.random.randint(jax.random.fold_in(own_key, axis), (), 0, length) for axis, length in enumerate(result.shape)]
    widest = result.shape.index(max(result.shape))
    neighbour = index_at[:widest] + [(index_at[widest] + 1) % result.shape[widest]] + index_at[widest + 1:]
    return result.at[tuple(index_at)].set(smallest).at[tuple(neighbour)].set(top_value)


def steps_of(stream_key, shape, pieces, low, top_value):
    factor_of = 1.0
    for position, blocks in pieces:
        steps = jax.random.uniform(jax.random.fold_in(jax.random.fold_in(stream_key, 6), position), (blocks,), jnp.float32, low / len(pieces), top_value / len(pieces))
        factor_of = factor_of * jnp.repeat(jnp.exp(steps), shape[position] // blocks).reshape((-1,) + (1,) * (len(shape) - 1 - position))
    return factor_of


def bell_draw(key, dims, scale, limit, cuts=(), kind=jnp.bfloat16):
    drawn = scale * jax.random.normal(key, dims, jnp.float32)
    if cuts:
        drawn = drawn * steps_of(key, dims, cuts, -0.22, 0.18)
    return jnp.clip(drawn, -limit, limit).astype(kind)


def setup_inputs(seed: int = 0, part: int = 0) -> dict:
    key_list = jax.random.split(jax.random.key(seed), 9)
    own_keys = jax.random.split(jax.random.fold_in(key_list[8], part), 9)
    correction = draw_correction(jax.random.fold_in(jax.random.fold_in(key_list[8], part), 71), part)
    left_blocks = bell_draw(own_keys[1], (PAIRS, BLK, BLK), BLK ** -0.5, 0.5, ((0, 16),), jnp.float32)
    right_blocks = bell_draw(own_keys[2], (K, BLK, BLK), (BLK * N_OPS * P_DEV // S_LOC) ** -0.5, 0.125, ((0, 4),), jnp.float32)
    send_sector = draw_send_sector(jax.random.fold_in(jax.random.fold_in(key_list[8], part), 71), part)
    pair_slot = draw_pair_slot(jax.random.fold_in(jax.random.fold_in(key_list[8], part), 71), part)
    pair_term = touch_ends(jax.random.randint(own_keys[5], (PAIRS,), 0, K_DEV), jax.random.fold_in(own_keys[5], 1), 0, K_DEV - 1).astype(jnp.int32)
    pair_dst = touch_ends(jax.random.randint(own_keys[6], (PAIRS,), 0, S_LOC), jax.random.fold_in(own_keys[6], 1), 0, S_LOC - 1).astype(jnp.int32)
    pair_live = draw_pair_live(jax.random.fold_in(jax.random.fold_in(key_list[8], part), 71), part)
    return {"correction": correction, "left_blocks": left_blocks, "right_blocks": right_blocks, "send_sector": send_sector, "pair_slot": pair_slot, "pair_term": pair_term, "pair_dst": pair_dst, "pair_live": pair_live}


epsilon = 1e-06
highest = lax.Precision.HIGHEST

def inverse_factor(gram_matrix):
    u_zero = jnp.sqrt(gram_matrix[0, 0])
    u_one = gram_matrix[0, 1] / u_zero
    u_two = gram_matrix[0, 2] / u_zero
    u_four = jnp.sqrt(gram_matrix[1, 1] - u_one * u_one)
    u_five = (gram_matrix[1, 2] - u_one * u_two) / u_four
    u_eight = jnp.sqrt(gram_matrix[2, 2] - u_two * u_two - u_five * u_five)
    v_zero = 1.0 / u_zero
    v_four = 1.0 / u_four
    v_eight = 1.0 / u_eight
    v_one = -u_one * v_zero * v_four
    v_five = -u_five * v_four * v_eight
    v_two = -(u_one * v_five + u_two * v_eight) * v_zero
    nought = jnp.zeros((), jnp.float32)
    return jnp.stack([jnp.stack([v_zero, v_one, v_two]), jnp.stack([nought, v_four, v_five]), jnp.stack([nought, nought, v_eight])])

def orthonormal(correction):
    entry_count = S * BLK * BLK
    gram_matrix = jnp.einsum('kabc,jabc->kj', correction, correction, precision=highest) / entry_count
    gram_matrix = gram_matrix + epsilon * jnp.eye(VECS, dtype=jnp.float32)
    inverse = inverse_factor(gram_matrix)
    return jnp.einsum('jabc,jk->kabc', correction, inverse, precision=highest)

def reference(correction, left_blocks, right_blocks, send_sector, pair_slot, pair_term, pair_dst, pair_live):
    holders = N_SEC * N_REP
    search_basis = orthonormal(correction)

    def device_step(sigma_blocks, device):
        owner = device // holders
        holder = device % holders
        start = (device * P_DEV).astype(jnp.int32)
        lefts = lax.dynamic_slice_in_dim(left_blocks, start, P_DEV, 0)
        slots = lax.dynamic_slice_in_dim(pair_slot, start, P_DEV, 0)
        terms = lax.dynamic_slice_in_dim(pair_term, start, P_DEV, 0) + owner * K_DEV
        targets = lax.dynamic_slice_in_dim(pair_dst, start, P_DEV, 0) + holder * S_LOC
        alive = lax.dynamic_slice_in_dim(pair_live, start, P_DEV, 0).astype(jnp.float32)
        sender = slots // CAP
        within = send_sector[sender, holder, slots % CAP]
        filled = (within >= 0).astype(jnp.float32)
        source = search_basis[:, sender * S_LOC + jnp.maximum(within, 0)]
        source = source * (filled * alive)[None, :, None, None]
        halfway = jnp.einsum('pij,kpjl->kpil', lefts, source, precision=highest)
        product = jnp.einsum('kpil,pml->kpim', halfway, right_blocks[terms], precision=highest)
        return (sigma_blocks.at[:, targets].add(product), None)
    sigma_blocks, unused = lax.scan(device_step, jnp.zeros(search_basis.shape, jnp.float32), jnp.arange(N_OPS * holders, dtype=jnp.int32))
    return (search_basis, sigma_blocks)
```

```python
import functools

import jax
import jax.numpy as jnp
from jax import lax
from jax.experimental import pallas as pl
from jax.experimental.pallas import tpu as pltpu
from jax.sharding import PartitionSpec as P

epsilon = 1e-06
vmem = pl.BlockSpec(memory_space=pltpu.VMEM)
smem = pl.BlockSpec(memory_space=pltpu.SMEM)
limit = pltpu.CompilerParams(vmem_limit_bytes=48 * 1024 * 1024)
pairs_of_three = ((0, 0), (0, 1), (0, 2), (1, 1), (1, 2), (2, 2))


def low_bit(mask):
    return mask & -mask


def swap(value, axes, size, mask):
    return lax.ppermute(value, axes, [(i, i ^ mask) for i in range(size)])


def holder_index():
    return lax.axis_index("sec") * lax.axis_size("rep") + lax.axis_index("rep")


def pack_kernel(holders, table_ref, correction_ref, *outs):
    vectors, _, rows, width = correction_ref.shape
    here = holder_index()
    tiles = []
    for i, j in pairs_of_three:
        total = jnp.sum(correction_ref[i] * correction_ref[j], axis=(0, 1))[None, :]
        total = jnp.sum(total, axis=1, keepdims=True)
        tiles.append(jnp.broadcast_to(total, (1, width)))
    tiles.append(jnp.zeros((2, width), jnp.float32))
    gram = jnp.concatenate(tiles, axis=0)
    for mask in range(holders):
        receiver = here ^ mask
        for slot in range(table_ref.shape[1]):
            sector = table_ref[receiver, slot]
            filled = (sector >= 0).astype(jnp.float32)
            sector = jnp.maximum(sector, 0)
            for vector in range(vectors):
                start = (vector * table_ref.shape[1] + slot) * rows
                outs[mask][start : start + rows, :] = correction_ref[vector, sector] * filled
        outs[mask][outs[mask].shape[0] - 8 :, :] = gram


def join_kernel(holders, cap, rows, *refs):
    received, outs = refs[:holders], refs[holders:]
    for vector, out in enumerate(outs):
        for mask in range(holders):
            part = received[mask][vector * cap * rows : (vector + 1) * cap * rows, :]
            out[mask * cap * rows : (mask + 1) * cap * rows, :] = part
    height = received[0].shape[0]
    gram = received[0][height - 8 :, :]
    for mask in range(1, holders):
        gram = gram + received[mask][height - 8 :, :]
    outs[0][holders * cap * rows :, :] = gram


def split(value):
    high = value.astype(jnp.bfloat16)
    return high, (value - high.astype(jnp.float32)).astype(jnp.bfloat16)


def operator_kernel(live_ref, left_ref, right_ref, high_ref, low_ref, right_high_ref, right_low_ref):
    width = left_ref.shape[1]

    def step(pair, carry):
        high, low = split(left_ref[pair] * live_ref[pair].astype(jnp.float32))
        high_ref[pair] = high
        low_ref[pair] = low
        return carry

    lax.fori_loop(0, left_ref.shape[0], step, 0, unroll=4)
    for term in range(right_ref.shape[0]):
        high, low = split(right_ref[term].T)
        right_high_ref[:, term * width : (term + 1) * width] = high
        right_low_ref[:, term * width : (term + 1) * width] = low


def inverse_rows(gram, entry_count):
    row = [gram[i : i + 1, :] / entry_count for i in range(6)]
    u_zero = jnp.sqrt(row[0] + epsilon)
    u_one = row[1] / u_zero
    u_two = row[2] / u_zero
    u_four = jnp.sqrt(row[3] + epsilon - u_one * u_one)
    u_five = (row[4] - u_one * u_two) / u_four
    u_eight = jnp.sqrt(row[5] + epsilon - u_two * u_two - u_five * u_five)
    v_zero = 1.0 / u_zero
    v_four = 1.0 / u_four
    v_eight = 1.0 / u_eight
    v_one = -u_one * v_zero * v_four
    v_five = -u_five * v_four * v_eight
    v_two = -(u_one * v_five + u_two * v_eight) * v_zero
    return [v_zero, v_one, v_two, v_four, v_five, v_eight]


def apply_kernel(vector, ops, rows, entry_count, *refs):
    refs = list(refs)
    slot_ref, term_ref, dst_ref = refs[:3]
    del refs[:3]
    pieces = [[refs.pop(0) for _ in range(ops)] for _ in range(vector + 1)]
    inverse_in = refs.pop(0) if vector else None
    high_ref, low_ref, right_high_ref, right_low_ref = refs[:4]
    del refs[:4]
    outs = [refs.pop(0) for _ in range(ops)]
    inverse_out = None if vector else refs.pop(0)
    source_ref, chosen_ref, total_ref = refs
    here, place = holder_index(), lax.axis_index("ops")
    slots, width, _ = source_ref.shape
    terms = right_high_ref.shape[1] // width
    count = slots * rows
    if vector:
        inverse = inverse_in[...]
    else:
        gram = pieces[0][0][count:, :]
        for mask in range(1, ops):
            gram = gram + pieces[0][mask][count:, :]
        inverse = jnp.concatenate(inverse_rows(gram, entry_count) + [gram[6:]], axis=0)
        inverse_out[...] = inverse
    factors = [
        inverse[i : i + 1, :] for i, (_, j) in enumerate(pairs_of_three) if j == vector
    ]
    for mask in range(ops):
        value = sum(pieces[j][mask][:count, :] * factors[j] for j in range(vector + 1))
        start = pl.multiple_of((place ^ mask) * rows, rows)
        source_ref[:, pl.ds(start, rows), :] = value.reshape(slots, rows, width)

    def right_step(slot, carry):
        high, low = split(source_ref[slot])
        product = jnp.dot(high, right_high_ref[...], preferred_element_type=jnp.float32)
        product += jnp.dot(low, right_high_ref[...], preferred_element_type=jnp.float32)
        product += jnp.dot(high, right_low_ref[...], preferred_element_type=jnp.float32)
        for term in range(terms):
            high, low = split(product[:, term * width : (term + 1) * width])
            chosen_ref[slot * terms + term, :, :width] = high
            chosen_ref[slot * terms + term, :, width:] = low
        return carry

    lax.fori_loop(0, slots, right_step, 0, unroll=2)
    total_ref[...] = jnp.zeros_like(total_ref)
    cap = slots // (lax.axis_size("sec") * lax.axis_size("rep"))

    def pair_step(pair, carry):
        slot = slot_ref[pair]
        slot = ((slot // cap) ^ here) * cap + slot % cap
        index = slot * terms + term_ref[pair]
        both = jnp.dot(high_ref[pair], chosen_ref[index], preferred_element_type=jnp.float32)
        rest = jnp.dot(low_ref[pair], chosen_ref[index, :, :width], preferred_element_type=jnp.float32)
        total_ref[dst_ref[pair]] += both[:, :width] + both[:, width:] + rest
        return carry

    lax.fori_loop(0, high_ref.shape[0], pair_step, 0, unroll=4)
    for mask in range(ops):
        start = pl.multiple_of((place ^ mask) * rows, rows)
        outs[mask][...] = total_ref[:, pl.ds(start, rows), :]


def local(
    correction, left_blocks, right_blocks, send_sector, pair_slot, pair_term, pair_dst, pair_live
):
    ops, holders = lax.axis_size("ops"), lax.axis_size(("sec", "rep"))
    vectors, sectors, rows, width = correction.shape
    cap = send_sector.shape[2]
    terms, pair_count = right_blocks.shape[0], left_blocks.shape[0]
    slots = holders * cap
    entry_count = float(sectors * holders * width * width)
    f32, bf16 = jnp.float32, jnp.bfloat16

    packed = pl.pallas_call(
        functools.partial(pack_kernel, holders),
        out_shape=[jax.ShapeDtypeStruct((vectors * cap * rows + 8, width), f32)] * holders,
        in_specs=[smem, vmem],
        out_specs=[vmem] * holders,
        compiler_params=limit,
        name="pack",
    )(send_sector[0], correction)
    received = [packed[0]] + [
        swap(packed[mask], ("sec", "rep"), holders, mask) for mask in range(1, holders)
    ]
    operators = pl.pallas_call(
        operator_kernel,
        out_shape=[jax.ShapeDtypeStruct((pair_count, width, width), bf16)] * 2
        + [jax.ShapeDtypeStruct((width, terms * width), bf16)] * 2,
        in_specs=[smem, vmem, vmem],
        out_specs=[vmem] * 4,
        compiler_params=limit,
        name="operators",
    )(pair_live, left_blocks, right_blocks)
    joined = pl.pallas_call(
        functools.partial(join_kernel, holders, cap, rows),
        out_shape=[
            jax.ShapeDtypeStruct((slots * rows + (0 if vector else 8), width), f32)
            for vector in range(vectors)
        ],
        in_specs=[vmem] * holders,
        out_specs=[vmem] * vectors,
        compiler_params=limit,
        name="join",
    )(*received)

    pieces = []
    for vector in range(vectors):
        piece = [joined[vector]] + [None] * (ops - 1)
        for mask in sorted(range(1, ops), key=lambda m: (bin(m).count("1"), -m)):
            bit = low_bit(mask)
            piece[mask] = swap(piece[mask ^ bit], "ops", ops, bit)
        pieces.append(piece)

    inverse = None
    sums = []
    for vector in range(vectors):
        arguments = [pair_slot, pair_term, pair_dst]
        for piece in pieces[: vector + 1]:
            arguments += piece
        if vector:
            arguments.append(inverse)
        arguments += operators
        out_shape = [jax.ShapeDtypeStruct((sectors, rows, width), f32)] * ops
        if not vector:
            out_shape = out_shape + [jax.ShapeDtypeStruct((8, width), f32)]
        parts = pl.pallas_call(
            functools.partial(apply_kernel, vector, ops, rows, entry_count),
            out_shape=out_shape,
            in_specs=[smem] * 3 + [vmem] * (len(arguments) - 3),
            out_specs=[vmem] * len(out_shape),
            scratch_shapes=[
                pltpu.VMEM((slots, width, width), f32),
                pltpu.VMEM((slots * terms, width, 2 * width), bf16),
                pltpu.VMEM((sectors, width, width), f32),
            ],
            compiler_params=limit,
            name="apply",
        )(*arguments)
        if not vector:
            inverse = parts[ops]
        parts = list(parts[:ops])
        for mask in sorted(range(1, ops), key=lambda m: (-bin(m).count("1"), -m)):
            bit = low_bit(mask)
            parts[mask ^ bit] = parts[mask ^ bit] + swap(parts[mask], "ops", ops, bit)
        sums.append(parts[0])

    column = inverse[:6, 0]
    search_basis = []
    for k in range(vectors):
        picked = [(i, a) for i, (a, b) in enumerate(pairs_of_three) if b == k]
        search_basis.append(sum(correction[a] * column[i] for i, a in picked))
    return (jnp.stack(search_basis), jnp.stack(sums))


def solution(mesh):
    placed = (
        P(None, ("groups", "sec", "rep"), "ops", None),
        P(("groups", "ops", "sec", "rep"), None, None),
        P(("groups", "ops"), None, None),
        P(("groups", "sec", "rep"), None, None),
        P(("groups", "ops", "sec", "rep")),
        P(("groups", "ops", "sec", "rep")),
        P(("groups", "ops", "sec", "rep")),
        P(("groups", "ops", "sec", "rep")),
    )
    return jax.shard_map(
        local,
        mesh=mesh,
        in_specs=placed,
        out_specs=(
            P(None, ("groups", "sec", "rep"), "ops", None),
            P(None, ("groups", "sec", "rep"), "ops", None),
        ),
        check_vma=False,
    )
```

```python
import functools

import jax
import jax.numpy as jnp
from jax import lax
from jax.experimental import pallas as pl
from jax.experimental.pallas import tpu as pltpu
from jax.sharding import PartitionSpec as P

epsilon = 1e-06
vmem = pl.BlockSpec(memory_space=pltpu.VMEM)
smem = pl.BlockSpec(memory_space=pltpu.SMEM)
anywhere = pl.BlockSpec(memory_space=pl.ANY)
limit = pltpu.CompilerParams(vmem_limit_bytes=48 * 1024 * 1024)
pairs_of_three = ((0, 0), (0, 1), (0, 2), (1, 1), (1, 2), (2, 2))
f32, bf16 = jnp.float32, jnp.bfloat16
dot = functools.partial(jnp.dot, preferred_element_type=f32)
parcels = ((0,), (1, 2))


def ring_order(ops):
    return [0] + list(range(1, ops, 2)) + list(range(ops - 2, 0, -2))


def ring_step(value, ops):
    order = ring_order(ops)
    return lax.ppermute(value, "ops", [(order[i - 1], order[i]) for i in range(ops)])


def shard_before(place, ops, steps):
    at = jnp.where(place % 2 == 1, (place + 1) // 2, (ops - place // 2) % ops)
    at = (at - steps + ops) % ops
    return jnp.where(at == 0, 0, jnp.where(at <= ops // 2, 2 * at - 1, 2 * (ops - at)))


def holder_index():
    return lax.axis_index("sec") * lax.axis_size("rep") + lax.axis_index("rep")


def follow(value, others):
    return lax.optimization_barrier((value,) + tuple(others))[0] if others else value


def split(value):
    high = value.astype(bf16)
    return high, (value - high.astype(f32)).astype(bf16)


def pack_kernel(holders, table_ref, correction_ref, *outs):
    rows, width = correction_ref.shape[2:]
    cap = table_ref.shape[0]
    here = holder_index()
    for turn, vectors in enumerate(parcels):
        for mask in range(holders):
            out = outs[turn * holders + mask]
            for slot in range(cap):
                sector = table_ref[slot, here ^ mask]
                filled = (sector >= 0).astype(f32)
                sector = jnp.maximum(sector, 0)
                for index, vector in enumerate(vectors):
                    start = (index * cap + slot) * rows
                    out[start : start + rows, :] = correction_ref[vector, sector] * filled
    tiles = []
    for i, j in pairs_of_three:
        total = jnp.sum(correction_ref[i] * correction_ref[j], axis=(0, 1))[None, :]
        total = jnp.sum(total, axis=1, keepdims=True)
        tiles.append(jnp.broadcast_to(total, (1, width)))
    tiles.append(jnp.zeros((2, width), f32))
    gram = jnp.concatenate(tiles, axis=0)
    for mask in range(holders):
        outs[mask][outs[mask].shape[0] - 8 :, :] = gram


def join_kernel(holders, block, with_gram, *refs):
    received, outs = refs[:holders], refs[holders + 1 :]
    for index, out in enumerate(outs):
        for sender, part_ref in enumerate(received):
            out[sender * block : (sender + 1) * block, :] = part_ref[index * block : (index + 1) * block, :]
    if with_gram:
        outs[0][holders * block :, :] = sum(ref[ref.shape[0] - 8 :, :] for ref in received)


def plan_kernel(pairs, sectors, cap, terms, packed_ref, plan_ref, next_ref):
    width = 5
    couples = plan_ref.shape[0] // width
    base = holder_index() * cap
    for sector in range(sectors):
        next_ref[sector] = 0

    def count_step(pair, carry):
        target = packed_ref[pair] & (sectors - 1)
        next_ref[target] += 1
        return carry

    def clear_step(couple, carry):
        for entry in range(3):
            plan_ref[width * couple + entry] = 0
        plan_ref[width * couple + 3] = -1
        plan_ref[width * couple + 4] = -1
        return carry

    lax.fori_loop(0, pairs, count_step, 0, unroll=4)
    lax.fori_loop(0, couples, clear_step, 0, unroll=4)
    start = jnp.int32(0)
    for sector in range(sectors):
        count = next_ref[sector]
        next_ref[sector] = start
        start = start + ((count + 1) & -2)

    def place_step(pair, carry):
        packed = packed_ref[pair]
        target = packed & (sectors - 1)
        packed = packed >> (sectors.bit_length() - 1)
        at = next_ref[target]
        next_ref[target] = at + 1
        first, side = (at >> 1) * width, at & 1
        slot = (packed >> (terms.bit_length() - 1)) ^ base
        plan_ref[first + side] = slot * terms + (packed & (terms - 1))
        plan_ref[first + 2] = target
        plan_ref[first + 3 + side] = pair
        return carry

    lax.fori_loop(0, pairs, place_step, 0, unroll=4)


def operator_kernel(plan_ref, live_ref, left_ref, right_ref, high_ref, low_ref, right_both_ref, right_low_ref):
    width, terms = left_ref.shape[1], right_ref.shape[0]

    def couple_step(couple, carry):
        for side in range(2):
            pair = plan_ref[5 * couple + 3 + side]
            kept = jnp.where(pair >= 0, 1, 0)
            pair = jnp.maximum(pair, 0)
            scale = (live_ref[pair] * kept).astype(f32)
            high, low = split(left_ref[pair] * scale)
            high_ref[couple, :, side * width : (side + 1) * width] = high
            low_ref[couple, :, side * width : (side + 1) * width] = low
        return carry

    lax.fori_loop(0, high_ref.shape[0], couple_step, 0, unroll=4)
    for term in range(terms):
        high, low = split(right_ref[term].T)
        columns = slice(term * width, (term + 1) * width)
        right_both_ref[:width, columns] = high
        right_both_ref[width:, columns] = high
        right_low_ref[:, columns] = low


def inverse_rows(gram, entry_count):
    row = [gram[i : i + 1, :] / entry_count for i in range(6)]
    u_zero = jnp.sqrt(row[0] + epsilon)
    u_one = row[1] / u_zero
    u_two = row[2] / u_zero
    u_four = jnp.sqrt(row[3] + epsilon - u_one * u_one)
    u_five = (row[4] - u_one * u_two) / u_four
    u_eight = jnp.sqrt(row[5] + epsilon - u_two * u_two - u_five * u_five)
    v_zero = 1.0 / u_zero
    v_four = 1.0 / u_four
    v_eight = 1.0 / u_eight
    v_one = -u_one * v_zero * v_four
    v_five = -u_five * v_four * v_eight
    v_two = -(u_one * v_five + u_two * v_eight) * v_zero
    return [v_zero, v_one, v_two, v_four, v_five, v_eight]


def apply_kernel(vector, ops, rows, entry_count, *refs):
    refs = list(refs)
    take = lambda count: [refs.pop(0) for _ in range(count)]
    plan_ref, high_ref, low_ref, right_both_ref, right_low_ref = take(5)
    pieces = [take(ops) for _ in range(vector + 1)]
    inverse_in = take(1)[0] if vector else None
    outs = take(ops)
    inverse_out = None if vector else take(1)[0]
    source_ref, chosen_ref, total_ref = refs
    place = lax.axis_index("ops")
    slots, width, _ = source_ref.shape
    terms = right_low_ref.shape[1] // width
    count = slots * rows
    if vector:
        inverse = inverse_in[...]
    else:
        gram = sum(piece[count:, :] for piece in pieces[0])
        inverse = jnp.concatenate(inverse_rows(gram, entry_count) + [gram[6:]], axis=0)
        inverse_out[...] = inverse
    for steps in range(ops):
        value = 0.0
        for earlier in range(vector + 1):
            at = pairs_of_three.index((earlier, vector))
            value += pieces[earlier][steps][:count, :] * inverse[at : at + 1, :]
        start = pl.multiple_of(shard_before(place, ops, steps) * rows, rows)
        source_ref[:, pl.ds(start, rows), :] = value.reshape(slots, rows, width)

    def right_step(slot, carry):
        high, low = split(source_ref[slot])
        product = dot(jnp.concatenate([high, low], axis=1), right_both_ref[...])
        product += dot(high, right_low_ref[...])
        for term in range(terms):
            high, low = split(product[:, term * width : (term + 1) * width])
            chosen_ref[slot * terms + term, :, :width] = high
            chosen_ref[slot * terms + term, :, width:] = low
        return carry

    lax.fori_loop(0, slots, right_step, 0, unroll=8)
    total_ref[...] = jnp.zeros_like(total_ref)

    def couple_step(couple, carry):
        first, second = plan_ref[5 * couple], plan_ref[5 * couple + 1]
        chosen = jnp.concatenate([chosen_ref[first], chosen_ref[second]], axis=0)
        both = dot(high_ref[couple], chosen)
        rest = dot(low_ref[couple], chosen[:, :width])
        total_ref[plan_ref[5 * couple + 2]] += both[:, :width] + both[:, width:] + rest
        return carry

    lax.fori_loop(0, high_ref.shape[0], couple_step, 0, unroll=True)
    for steps in range(ops):
        start = pl.multiple_of(shard_before(place, ops, steps) * rows, rows)
        outs[steps][...] = total_ref[:, pl.ds(start, rows), :]


def basis_kernel(inverse_ref, correction_ref, out_ref):
    inverse = inverse_ref[...]
    for k in range(out_ref.shape[0]):
        picked = [(i, j) for i, (j, column) in enumerate(pairs_of_three) if column == k]
        out_ref[k] = sum(correction_ref[j] * inverse[i : i + 1, :] for i, j in picked)


def finish_kernel(*refs):
    out, terms = refs[-1], refs[:-1]
    for vector in range(out.shape[0]):
        out[vector] = terms[2 * vector][...] + terms[2 * vector + 1][...]


def call(kernel, out, inputs, specs, out_specs, name, scratch=()):
    return pl.pallas_call(
        kernel,
        out_shape=[jax.ShapeDtypeStruct(shape, dtype) for shape, dtype in out],
        in_specs=specs,
        out_specs=out_specs,
        scratch_shapes=list(scratch),
        compiler_params=limit,
        name=name,
    )(*inputs)


def local(
    correction, left_blocks, right_blocks, send_sector, pair_slot, pair_term, pair_dst, pair_live
):
    ops, holders = lax.axis_size("ops"), lax.axis_size(("sec", "rep"))
    vectors, sectors, rows, width = correction.shape
    cap = send_sector.shape[2]
    terms, pairs = right_blocks.shape[0], left_blocks.shape[0]
    slots, block = holders * cap, cap * rows
    entry_count = float(sectors * holders * width * width)
    couples = (pairs + min(pairs, sectors)) // 2

    packed = call(
        functools.partial(pack_kernel, holders),
        [
            ((len(parcel) * block + (0 if turn else 8), width), f32)
            for turn, parcel in enumerate(parcels)
            for _ in range(holders)
        ],
        (send_sector[0].T, correction),
        [smem, vmem],
        [vmem] * (len(parcels) * holders),
        "pack",
    )
    joined = []
    received = []
    for turn in range(len(parcels)):
        mine = list(packed[turn * holders : (turn + 1) * holders])
        for mask in range(holders - 1, 0, -1):
            mine[mask] = lax.ppermute(
                mine[mask], ("sec", "rep"), [(i, i ^ mask) for i in range(holders)]
            )
        received.append(mine)
    (plan,) = call(
        functools.partial(plan_kernel, pairs, sectors, cap, terms),
        [((5 * couples,), jnp.int32)],
        ((pair_slot * terms + pair_term) * sectors + pair_dst,),
        [smem],
        [smem],
        "plan",
        [pltpu.SMEM((sectors,), jnp.int32)],
    )
    for turn, parcel in enumerate(parcels):
        joined += call(
            functools.partial(join_kernel, holders, block, turn == 0),
            [
                ((slots * rows + (8 if turn == 0 and index == 0 else 0), width), f32)
                for index in range(len(parcel))
            ],
            received[turn] + [plan],
            [vmem] * holders + [anywhere],
            [vmem] * len(parcel),
            "join",
        )
    high, low, right_both, right_low = call(
        operator_kernel,
        [
            ((couples, width, 2 * width), bf16),
            ((couples, width, 2 * width), bf16),
            ((2 * width, terms * width), bf16),
            ((width, terms * width), bf16),
        ],
        (plan, pair_live, left_blocks, right_blocks),
        [smem] * 2 + [vmem] * 2,
        [vmem] * 4,
        "operators",
    )

    pieces = [[value] for value in joined]
    for step in range(1, ops):
        for vector in range(vectors):
            value = pieces[vector][-1]
            if vector == 0 and step == 2:
                value = follow(value, (right_low,))
            pieces[vector].append(ring_step(value, ops))

    inverse = None
    sums = []
    for vector in range(vectors):
        arguments = [plan, high, low, right_both, right_low]
        arguments += sum(pieces[: vector + 1], [])
        arguments += [inverse] if vector else []
        out = [((sectors, rows, width), f32)] * ops + ([] if vector else [((8, width), f32)])
        parts = call(
            functools.partial(apply_kernel, vector, ops, rows, entry_count),
            out,
            arguments,
            [smem] + [vmem] * (len(arguments) - 1),
            [vmem] * len(out),
            "apply",
            [
                pltpu.VMEM((slots, width, width), f32),
                pltpu.VMEM((slots * terms, width, 2 * width), bf16),
                pltpu.VMEM((sectors, width, width), f32),
            ],
        )
        if vector == 0:
            inverse = parts[ops]
            (search_basis,) = call(
                basis_kernel, [(correction.shape, f32)], (inverse, correction), [vmem] * 2, [vmem], "basis"
            )
        total = parts[1]
        for step in range(2, ops):
            if vector == 1 and step == 2:
                total = follow(total, (search_basis,))
            total = parts[step] + ring_step(total, ops)
        sums += [parts[0], ring_step(total, ops)]

    (sigma_blocks,) = call(
        finish_kernel,
        [(correction.shape, f32)],
        sums,
        [vmem] * len(sums),
        [vmem],
        "finish",
    )
    return (search_basis, sigma_blocks)


def solution(mesh):
    placed = (
        P(None, ("groups", "sec", "rep"), "ops", None),
        P(("groups", "ops", "sec", "rep"), None, None),
        P(("groups", "ops"), None, None),
        P(("groups", "sec", "rep"), None, None),
        P(("groups", "ops", "sec", "rep")),
        P(("groups", "ops", "sec", "rep")),
        P(("groups", "ops", "sec", "rep")),
        P(("groups", "ops", "sec", "rep")),
    )
    return jax.shard_map(
        local,
        mesh=mesh,
        in_specs=placed,
        out_specs=(
            P(None, ("groups", "sec", "rep"), "ops", None),
            P(None, ("groups", "sec", "rep"), "ops", None),
        ),
        check_vma=False,
    )
```

```python
import functools

import jax
import jax.numpy as jnp
from jax import lax
from jax.experimental import pallas as pl
from jax.experimental.pallas import tpu as pltpu
from jax.sharding import PartitionSpec as P

epsilon = 1e-06
vmem = pl.BlockSpec(memory_space=pltpu.VMEM)
smem = pl.BlockSpec(memory_space=pltpu.SMEM)
anywhere = pl.BlockSpec(memory_space=pl.ANY)
limit = pltpu.CompilerParams(vmem_limit_bytes=48 * 1024 * 1024)
pairs_of_three = ((0, 0), (0, 1), (0, 2), (1, 1), (1, 2), (2, 2))
f32, bf16 = jnp.float32, jnp.bfloat16
dot = functools.partial(jnp.dot, preferred_element_type=f32)


def ring_order(ops):
    return [0] + list(range(1, ops, 2)) + list(range(ops - 2, 0, -2))


def ring_step(value, ops):
    order = ring_order(ops)
    return lax.ppermute(value, "ops", [(order[i - 1], order[i]) for i in range(ops)])


def shard_before(place, ops, steps):
    at = jnp.where(place % 2 == 1, (place + 1) // 2, (ops - place // 2) % ops)
    at = (at - steps + ops) % ops
    return jnp.where(at == 0, 0, jnp.where(at <= ops // 2, 2 * at - 1, 2 * (ops - at)))


def holder_index():
    return lax.axis_index("sec") * lax.axis_size("rep") + lax.axis_index("rep")


def follow(value, others):
    return lax.optimization_barrier((value,) + tuple(others))[0] if others else value


def split(value):
    high = value.astype(bf16)
    return high, (value - high.astype(f32)).astype(bf16)


def pack_kernel(holders, table_ref, correction_ref, *outs):
    vectors, _, rows, width = correction_ref.shape
    cap = table_ref.shape[0]
    here = holder_index()
    for mask, out in enumerate(outs):
        for slot in range(cap):
            sector = table_ref[slot, here ^ mask]
            filled = (sector >= 0).astype(f32)
            sector = jnp.maximum(sector, 0)
            for vector in range(vectors):
                start = (vector * cap + slot) * rows
                out[start : start + rows, :] = correction_ref[vector, sector] * filled
    tiles = []
    for i, j in pairs_of_three:
        total = jnp.sum(correction_ref[i] * correction_ref[j], axis=(0, 1))[None, :]
        total = jnp.sum(total, axis=1, keepdims=True)
        tiles.append(jnp.broadcast_to(total, (1, width)))
    tiles.append(jnp.zeros((2, width), f32))
    gram = jnp.concatenate(tiles, axis=0)
    for out in outs:
        out[out.shape[0] - 8 :, :] = gram


def join_kernel(holders, block, *refs):
    received, outs = refs[:holders], refs[holders + 1 :]
    for index, out in enumerate(outs):
        for sender, part_ref in enumerate(received):
            out[sender * block : (sender + 1) * block, :] = part_ref[index * block : (index + 1) * block, :]
    outs[0][holders * block :, :] = sum(ref[ref.shape[0] - 8 :, :] for ref in received)


def plan_kernel(pairs, sectors, cap, terms, packed_ref, plan_ref, next_ref):
    width = 5
    couples = plan_ref.shape[0] // width
    base = holder_index() * cap
    for sector in range(sectors):
        next_ref[sector] = 0

    def count_step(pair, carry):
        target = packed_ref[pair] & (sectors - 1)
        next_ref[target] += 1
        return carry

    def clear_step(couple, carry):
        for entry in range(3):
            plan_ref[width * couple + entry] = 0
        plan_ref[width * couple + 3] = -1
        plan_ref[width * couple + 4] = -1
        return carry

    lax.fori_loop(0, pairs, count_step, 0, unroll=4)
    lax.fori_loop(0, couples, clear_step, 0, unroll=4)
    start = jnp.int32(0)
    for sector in range(sectors):
        count = next_ref[sector]
        next_ref[sector] = start
        start = start + ((count + 1) & -2)

    def place_step(pair, carry):
        packed = packed_ref[pair]
        target = packed & (sectors - 1)
        packed = packed >> (sectors.bit_length() - 1)
        at = next_ref[target]
        next_ref[target] = at + 1
        first, side = (at >> 1) * width, at & 1
        slot = (packed >> (terms.bit_length() - 1)) ^ base
        plan_ref[first + side] = slot * terms + (packed & (terms - 1))
        plan_ref[first + 2] = target
        plan_ref[first + 3 + side] = pair
        return carry

    lax.fori_loop(0, pairs, place_step, 0, unroll=4)


def operator_kernel(plan_ref, live_ref, left_ref, right_ref, *refs):
    high_ref, low_ref, right_both_ref, right_low_ref = refs[-4:]
    width, terms = left_ref.shape[1], right_ref.shape[0]

    def couple_step(couple, carry):
        for side in range(2):
            pair = plan_ref[5 * couple + 3 + side]
            kept = jnp.where(pair >= 0, 1, 0)
            pair = jnp.maximum(pair, 0)
            scale = (live_ref[pair] * kept).astype(f32)
            high, low = split(left_ref[pair] * scale)
            high_ref[couple, :, side * width : (side + 1) * width] = high
            low_ref[couple, :, side * width : (side + 1) * width] = low
        return carry

    lax.fori_loop(0, high_ref.shape[0], couple_step, 0, unroll=4)
    for term in range(terms):
        high, low = split(right_ref[term].T)
        columns = slice(term * width, (term + 1) * width)
        right_both_ref[:width, columns] = high
        right_both_ref[width:, columns] = high
        right_low_ref[:, columns] = low


def inverse_rows(gram, entry_count):
    row = [gram[i : i + 1, :] / entry_count for i in range(6)]
    u_zero = jnp.sqrt(row[0] + epsilon)
    u_one = row[1] / u_zero
    u_two = row[2] / u_zero
    u_four = jnp.sqrt(row[3] + epsilon - u_one * u_one)
    u_five = (row[4] - u_one * u_two) / u_four
    u_eight = jnp.sqrt(row[5] + epsilon - u_two * u_two - u_five * u_five)
    v_zero = 1.0 / u_zero
    v_four = 1.0 / u_four
    v_eight = 1.0 / u_eight
    v_one = -u_one * v_zero * v_four
    v_five = -u_five * v_four * v_eight
    v_two = -(u_one * v_five + u_two * v_eight) * v_zero
    return [v_zero, v_one, v_two, v_four, v_five, v_eight]


def apply_kernel(vector, holders, ops, rows, entry_count, *refs):
    refs = list(refs)
    take = lambda count: [refs.pop(0) for _ in range(count)]
    plan_ref, high_ref, low_ref, right_both_ref, right_low_ref = take(5)
    near = take(holders)
    pieces = [take(ops - 1) for _ in range(vector + 1)]
    inverse_in = take(1)[0] if vector else None
    outs = take(ops)
    inverse_out = None if vector else take(1)[0]
    source_ref, chosen_ref, total_ref = refs
    place = lax.axis_index("ops")
    slots, width, _ = source_ref.shape
    terms = right_low_ref.shape[1] // width
    count = slots * rows
    if vector:
        inverse = inverse_in[...]
    else:
        gram = sum(ref[ref.shape[0] - 8 :, :] for ref in near + pieces[0])
        inverse = jnp.concatenate(inverse_rows(gram, entry_count) + [gram[6:]], axis=0)
        inverse_out[...] = inverse
    factors = [inverse[i : i + 1, :] for i, (_, column) in enumerate(pairs_of_three) if column == vector]
    cap = slots // holders
    block = cap * rows
    start = pl.multiple_of(place * rows, rows)
    for sender, ref in enumerate(near):
        value = sum(ref[j * block : (j + 1) * block, :] * factor for j, factor in enumerate(factors))
        source_ref[sender * cap : (sender + 1) * cap, pl.ds(start, rows), :] = value.reshape(cap, rows, width)
    for steps in range(1, ops):
        value = sum(pieces[j][steps - 1][:count, :] * factor for j, factor in enumerate(factors))
        start = pl.multiple_of(shard_before(place, ops, steps) * rows, rows)
        source_ref[:, pl.ds(start, rows), :] = value.reshape(slots, rows, width)

    def right_step(slot, carry):
        high, low = split(source_ref[slot])
        product = dot(jnp.concatenate([high, low], axis=1), right_both_ref[...])
        product += dot(high, right_low_ref[...])
        for term in range(terms):
            high, low = split(product[:, term * width : (term + 1) * width])
            chosen_ref[slot * terms + term, :, :width] = high
            chosen_ref[slot * terms + term, :, width:] = low
        return carry

    lax.fori_loop(0, slots, right_step, 0, unroll=8)
    total_ref[...] = jnp.zeros_like(total_ref)

    def couple_step(couple, carry):
        first, second = plan_ref[5 * couple], plan_ref[5 * couple + 1]
        chosen = jnp.concatenate([chosen_ref[first], chosen_ref[second]], axis=0)
        both = dot(high_ref[couple], chosen)
        rest = dot(low_ref[couple], chosen[:, :width])
        total_ref[plan_ref[5 * couple + 2]] += both[:, :width] + both[:, width:] + rest
        return carry

    lax.fori_loop(0, high_ref.shape[0], couple_step, 0, unroll=True)
    for steps in range(ops):
        start = pl.multiple_of(shard_before(place, ops, steps) * rows, rows)
        outs[steps][...] = total_ref[:, pl.ds(start, rows), :]


def basis_kernel(inverse_ref, correction_ref, out_ref):
    inverse = inverse_ref[...]
    for k in range(out_ref.shape[0]):
        picked = [(i, j) for i, (j, column) in enumerate(pairs_of_three) if column == k]
        out_ref[k] = sum(correction_ref[j] * inverse[i : i + 1, :] for i, j in picked)


def part_kernel(kept_ref, arrived_ref, out_ref):
    out_ref[...] = kept_ref[...] + arrived_ref[...]


def finish_kernel(counts, *refs):
    refs, out = list(refs[:-1]), refs[-1]
    for vector, count in enumerate(counts):
        out[vector] = sum(refs.pop(0)[...] for _ in range(count))


small = pl.CostEstimate(flops=1, bytes_accessed=1, transcendentals=0)


def call(kernel, out, inputs, specs, out_specs, name, scratch=(), cost=None):
    return pl.pallas_call(
        kernel,
        out_shape=[jax.ShapeDtypeStruct(shape, dtype) for shape, dtype in out],
        in_specs=specs,
        out_specs=out_specs,
        scratch_shapes=list(scratch),
        compiler_params=limit,
        cost_estimate=cost,
        name=name,
    )(*inputs)


def local(
    correction, left_blocks, right_blocks, send_sector, pair_slot, pair_term, pair_dst, pair_live
):
    ops, holders = lax.axis_size("ops"), lax.axis_size(("sec", "rep"))
    vectors, sectors, rows, width = correction.shape
    cap = send_sector.shape[2]
    terms, pairs = right_blocks.shape[0], left_blocks.shape[0]
    slots, block = holders * cap, cap * rows
    entry_count = float(sectors * holders * width * width)
    couples = (pairs + min(pairs, sectors)) // 2

    packed = call(
        functools.partial(pack_kernel, holders),
        [((vectors * block + 8, width), f32)] * holders,
        (send_sector[0].T, correction),
        [smem, vmem],
        [vmem] * holders,
        "pack",
    )
    order = ring_order(ops)
    received = [
        lax.ppermute(
            packed[mask],
            ("ops", "sec", "rep"),
            [
                (order[i - 1] * holders + e, order[i] * holders + (e ^ mask))
                for i in range(ops)
                for e in range(holders)
            ],
        )
        for mask in range(holders)
    ]
    near = [packed[0]] + [
        lax.ppermute(packed[mask], ("sec", "rep"), [(e, e ^ mask) for e in range(holders)])
        for mask in range(1, holders)
    ]
    (plan,) = call(
        functools.partial(plan_kernel, pairs, sectors, cap, terms),
        [((5 * couples,), jnp.int32)],
        ((pair_slot * terms + pair_term) * sectors + pair_dst,),
        [smem],
        [smem],
        "plan",
        [pltpu.SMEM((sectors,), jnp.int32)],
    )
    high, low, right_both, right_low = call(
        operator_kernel,
        [
            ((couples, width, 2 * width), bf16),
            ((couples, width, 2 * width), bf16),
            ((2 * width, terms * width), bf16),
            ((width, terms * width), bf16),
        ],
        (plan, pair_live, left_blocks, right_blocks),
        [smem] * 2 + [vmem] * 2,
        [vmem] * 4,
        "operators",
    )

    joined = call(
        functools.partial(join_kernel, holders, block),
        [((slots * rows + (0 if vector else 8), width), f32) for vector in range(vectors)],
        received + [right_low],
        [vmem] * holders + [anywhere],
        [vmem] * vectors,
        "join",
    )
    pieces = [[value] for value in joined]
    for step in range(2, ops):
        for vector in range(vectors):
            value = pieces[vector][-1]
            if vector == 2 and step == 3:
                value = follow(value, near[1:])
            pieces[vector].append(ring_step(value, ops))

    inverse = None
    sums = []
    for vector in range(vectors):
        arguments = [plan, high, low, right_both, right_low]
        arguments += near + sum(pieces[: vector + 1], [])
        arguments += [inverse] if vector else []
        out = [((sectors, rows, width), f32)] * ops + ([] if vector else [((8, width), f32)])
        parts = call(
            functools.partial(apply_kernel, vector, holders, ops, rows, entry_count),
            out,
            arguments,
            [smem] + [vmem] * (len(arguments) - 1),
            [vmem] * len(out),
            "apply",
            [
                pltpu.VMEM((slots, width, width), f32),
                pltpu.VMEM((slots * terms, width, 2 * width), bf16),
                pltpu.VMEM((sectors, width, width), f32),
            ],
            small,
        )
        if vector == 0:
            inverse = parts[ops]
            (search_basis,) = call(
                basis_kernel, [(correction.shape, f32)], (inverse, correction), [vmem] * 2, [vmem], "basis"
            )
        total = parts[1]
        for step in range(2, ops):
            if vector == 2 and step == 3:
                total = follow(total, (search_basis,))
            total = parts[step] + ring_step(total, ops)
        ends = [parts[0], ring_step(total, ops)]
        if vector < 2:
            ends = list(call(
                part_kernel, [((sectors, rows, width), f32)], ends, [vmem] * 2, [vmem], "part", cost=small)
            )
        sums.append(ends)
    (sigma_blocks,) = call(
        functools.partial(finish_kernel, [len(ends) for ends in sums]),
        [(correction.shape, f32)],
        sum(sums, []),
        [vmem] * sum(len(ends) for ends in sums),
        [vmem],
        "finish",
    )
    return (search_basis, sigma_blocks)


def solution(mesh):
    placed = (
        P(None, ("groups", "sec", "rep"), "ops", None),
        P(("groups", "ops", "sec", "rep"), None, None),
        P(("groups", "ops"), None, None),
        P(("groups", "sec", "rep"), None, None),
        P(("groups", "ops", "sec", "rep")),
        P(("groups", "ops", "sec", "rep")),
        P(("groups", "ops", "sec", "rep")),
        P(("groups", "ops", "sec", "rep")),
    )
    return jax.shard_map(
        local,
        mesh=mesh,
        in_specs=placed,
        out_specs=(
            P(None, ("groups", "sec", "rep"), "ops", None),
            P(None, ("groups", "sec", "rep"), "ops", None),
        ),
        check_vma=False,
    )
```

```python
import functools

import jax
import jax.numpy as jnp
from jax import lax
from jax.experimental import pallas as pl
from jax.experimental.pallas import tpu as pltpu
from jax.sharding import PartitionSpec as P

epsilon = 1e-06
vmem = pl.BlockSpec(memory_space=pltpu.VMEM)
smem = pl.BlockSpec(memory_space=pltpu.SMEM)
hbm = pl.BlockSpec(memory_space=pltpu.HBM)
anywhere = pl.BlockSpec(memory_space=pl.ANY)
limit = pltpu.CompilerParams(vmem_limit_bytes=48 * 1024 * 1024)
pairs_of_three = ((0, 0), (0, 1), (0, 2), (1, 1), (1, 2), (2, 2))
f32, bf16 = jnp.float32, jnp.bfloat16
dot = functools.partial(jnp.dot, preferred_element_type=f32)


def ring_order(ops):
    return [0] + list(range(1, ops, 2)) + list(range(ops - 2, 0, -2))


def ring_step(value, ops):
    order = ring_order(ops)
    return lax.ppermute(value, "ops", [(order[i - 1], order[i]) for i in range(ops)])


def shard_before(place, ops, steps):
    at = jnp.where(place % 2 == 1, (place + 1) // 2, (ops - place // 2) % ops)
    at = (at - steps + ops) % ops
    return jnp.where(at == 0, 0, jnp.where(at <= ops // 2, 2 * at - 1, 2 * (ops - at)))


def holder_index():
    return lax.axis_index("sec") * lax.axis_size("rep") + lax.axis_index("rep")


def main_memory(value):
    return pltpu.with_memory_space_constraint(value, pltpu.HBM)


def follow(value, others):
    return lax.optimization_barrier((value,) + tuple(others))[0] if others else value


def split(value):
    high = value.astype(bf16)
    return high, (value - high.astype(f32)).astype(bf16)


def pack_kernel(table_in, correction_in, *refs):
    *outs, table_ref, correction_ref, table_sem, correction_sem = refs
    table_copy = pltpu.make_async_copy(table_in, table_ref, table_sem)
    correction_copy = pltpu.make_async_copy(correction_in, correction_ref, correction_sem)
    correction_copy.start()
    table_copy.start()
    table_copy.wait()
    correction_copy.wait()
    vectors, _, rows, width = correction_ref.shape
    cap = table_ref.shape[0]
    here = holder_index()
    for mask, out in enumerate(outs):
        for slot in range(cap):
            sector = table_ref[slot, here ^ mask]
            filled = (sector >= 0).astype(f32)
            sector = jnp.maximum(sector, 0)
            for vector in range(vectors):
                start = (vector * cap + slot) * rows
                out[start : start + rows, :] = correction_ref[vector, sector] * filled
    tiles = []
    for i, j in pairs_of_three:
        total = jnp.sum(correction_ref[i] * correction_ref[j], axis=(0, 1))[None, :]
        total = jnp.sum(total, axis=1, keepdims=True)
        tiles.append(jnp.broadcast_to(total, (1, width)))
    tiles.append(jnp.zeros((2, width), f32))
    gram = jnp.concatenate(tiles, axis=0)
    for out in outs:
        out[out.shape[0] - 8 :, :] = gram


def join_kernel(holders, block, *refs):
    received, outs = refs[:holders], refs[holders + 1 :]
    for index, out in enumerate(outs):
        for sender, part_ref in enumerate(received):
            out[sender * block : (sender + 1) * block, :] = part_ref[index * block : (index + 1) * block, :]
    outs[0][holders * block :, :] = sum(ref[ref.shape[0] - 8 :, :] for ref in received)


def plan_kernel(pairs, sectors, cap, terms, packed_ref, plan_ref, next_ref):
    width = 5
    couples = plan_ref.shape[0] // width
    base = holder_index() * cap
    for sector in range(sectors):
        next_ref[sector] = 0

    def count_step(pair, carry):
        target = packed_ref[pair] & (sectors - 1)
        next_ref[target] += 1
        return carry

    def clear_step(couple, carry):
        for entry in range(3):
            plan_ref[width * couple + entry] = 0
        plan_ref[width * couple + 3] = -1
        plan_ref[width * couple + 4] = -1
        return carry

    lax.fori_loop(0, pairs, count_step, 0, unroll=4)
    lax.fori_loop(0, couples, clear_step, 0, unroll=4)
    start = jnp.int32(0)
    for sector in range(sectors):
        count = next_ref[sector]
        next_ref[sector] = start
        start = start + ((count + 1) & -2)

    def place_step(pair, carry):
        packed = packed_ref[pair]
        target = packed & (sectors - 1)
        packed = packed >> (sectors.bit_length() - 1)
        at = next_ref[target]
        next_ref[target] = at + 1
        first, side = (at >> 1) * width, at & 1
        slot = (packed >> (terms.bit_length() - 1)) ^ base
        plan_ref[first + side] = slot * terms + (packed & (terms - 1))
        plan_ref[first + 2] = target
        plan_ref[first + 3 + side] = pair
        return carry

    lax.fori_loop(0, pairs, place_step, 0, unroll=4)


def operator_kernel(plan_ref, live_in, left_in, right_in, *refs):
    high_ref, low_ref, right_both_ref, right_low_ref, live_ref, left_ref, right_ref, live_sem, left_sem, right_sem = refs
    width, terms = left_ref.shape[1], right_ref.shape[0]
    right_copy = pltpu.make_async_copy(right_in, right_ref, right_sem)
    live_copy = pltpu.make_async_copy(live_in, live_ref, live_sem)
    left_copy = pltpu.make_async_copy(left_in, left_ref, left_sem)
    right_copy.start()
    live_copy.start()
    left_copy.start()
    right_copy.wait()
    for term in range(terms):
        high, low = split(right_ref[term].T)
        columns = slice(term * width, (term + 1) * width)
        right_both_ref[:width, columns] = high
        right_both_ref[width:, columns] = high
        right_low_ref[:, columns] = low
    live_copy.wait()
    left_copy.wait()

    def couple_step(couple, carry):
        for side in range(2):
            pair = plan_ref[5 * couple + 3 + side]
            kept = jnp.where(pair >= 0, 1, 0)
            pair = jnp.maximum(pair, 0)
            scale = (live_ref[pair] * kept).astype(f32)
            high, low = split(left_ref[pair] * scale)
            high_ref[couple, :, side * width : (side + 1) * width] = high
            low_ref[couple, :, side * width : (side + 1) * width] = low
        return carry

    lax.fori_loop(0, high_ref.shape[0], couple_step, 0, unroll=4)


def inverse_rows(gram, entry_count):
    row = [gram[i : i + 1, :] / entry_count for i in range(6)]
    u_zero = jnp.sqrt(row[0] + epsilon)
    u_one = row[1] / u_zero
    u_two = row[2] / u_zero
    u_four = jnp.sqrt(row[3] + epsilon - u_one * u_one)
    u_five = (row[4] - u_one * u_two) / u_four
    u_eight = jnp.sqrt(row[5] + epsilon - u_two * u_two - u_five * u_five)
    v_zero = 1.0 / u_zero
    v_four = 1.0 / u_four
    v_eight = 1.0 / u_eight
    v_one = -u_one * v_zero * v_four
    v_five = -u_five * v_four * v_eight
    v_two = -(u_one * v_five + u_two * v_eight) * v_zero
    return [v_zero, v_one, v_two, v_four, v_five, v_eight]


def apply_kernel(vector, holders, ops, rows, entry_count, *refs):
    refs = list(refs)
    take = lambda count: [refs.pop(0) for _ in range(count)]
    plan_ref, high_ref, low_ref, right_both_ref, right_low_ref = take(5)
    near = take(holders)
    pieces = [take(ops - 1) for _ in range(vector + 1)]
    inverse_in = take(1)[0] if vector else None
    outs = take(ops)
    inverse_out = None if vector else take(1)[0]
    source_ref, chosen_ref, total_ref = refs
    place = lax.axis_index("ops")
    slots, width, _ = source_ref.shape
    terms = right_low_ref.shape[1] // width
    count = slots * rows
    if vector:
        inverse = inverse_in[...]
    else:
        gram = sum(ref[ref.shape[0] - 8 :, :] for ref in near + pieces[0])
        inverse = jnp.concatenate(inverse_rows(gram, entry_count) + [gram[6:]], axis=0)
        inverse_out[...] = inverse
    factors = [inverse[i : i + 1, :] for i, (_, column) in enumerate(pairs_of_three) if column == vector]
    cap = slots // holders
    block = cap * rows
    start = pl.multiple_of(place * rows, rows)
    for sender, ref in enumerate(near):
        value = sum(ref[j * block : (j + 1) * block, :] * factor for j, factor in enumerate(factors))
        source_ref[sender * cap : (sender + 1) * cap, pl.ds(start, rows), :] = value.reshape(cap, rows, width)
    for steps in range(1, ops):
        value = sum(pieces[j][steps - 1][:count, :] * factor for j, factor in enumerate(factors))
        start = pl.multiple_of(shard_before(place, ops, steps) * rows, rows)
        source_ref[:, pl.ds(start, rows), :] = value.reshape(slots, rows, width)

    def right_step(slot, carry):
        high, low = split(source_ref[slot])
        product = dot(jnp.concatenate([high, low], axis=1), right_both_ref[...])
        product += dot(high, right_low_ref[...])
        for term in range(terms):
            high, low = split(product[:, term * width : (term + 1) * width])
            chosen_ref[slot * terms + term, :, :width] = high
            chosen_ref[slot * terms + term, :, width:] = low
        return carry

    lax.fori_loop(0, slots, right_step, 0, unroll=8)
    total_ref[...] = jnp.zeros_like(total_ref)

    def couple_step(couple, carry):
        first, second = plan_ref[5 * couple], plan_ref[5 * couple + 1]
        chosen = jnp.concatenate([chosen_ref[first], chosen_ref[second]], axis=0)
        both = dot(high_ref[couple], chosen)
        rest = dot(low_ref[couple], chosen[:, :width])
        total_ref[plan_ref[5 * couple + 2]] += both[:, :width] + both[:, width:] + rest
        return carry

    lax.fori_loop(0, high_ref.shape[0], couple_step, 0, unroll=True)
    for steps in range(ops):
        start = pl.multiple_of(shard_before(place, ops, steps) * rows, rows)
        outs[steps][...] = total_ref[:, pl.ds(start, rows), :]


def part_kernel(vector, kept_ref, arrived_ref, _, out, sum_ref, sum_sem):
    sum_ref[...] = kept_ref[...] + arrived_ref[...]
    copy = pltpu.make_async_copy(sum_ref, out.at[vector], sum_sem)
    copy.start()
    copy.wait()


def part_and_basis_kernel(kept_ref, arrived_ref, inverse_ref, correction_ref, out, basis_ref, sum_ref, sum_sem):
    sum_ref[...] = kept_ref[...] + arrived_ref[...]
    copy = pltpu.make_async_copy(sum_ref, out.at[0], sum_sem)
    copy.start()
    inverse = inverse_ref[...]
    for k in range(basis_ref.shape[0]):
        picked = [(i, j) for i, (j, column) in enumerate(pairs_of_three) if column == k]
        basis_ref[k] = sum(correction_ref[j] * inverse[i : i + 1, :] for i, j in picked)
    copy.wait()


small = pl.CostEstimate(flops=1, bytes_accessed=1, transcendentals=0)


def call(kernel, out, inputs, specs, out_specs, name, scratch=(), cost=None, aliases={}):
    return pl.pallas_call(
        kernel,
        out_shape=[jax.ShapeDtypeStruct(shape, dtype) for shape, dtype in out],
        in_specs=specs,
        out_specs=out_specs,
        scratch_shapes=list(scratch),
        compiler_params=limit,
        cost_estimate=cost,
        input_output_aliases=aliases,
        name=name,
    )(*inputs)


def local(
    correction, left_blocks, right_blocks, send_sector, pair_slot, pair_term, pair_dst, pair_live
):
    ops, holders = lax.axis_size("ops"), lax.axis_size(("sec", "rep"))
    vectors, sectors, rows, width = correction.shape
    cap = send_sector.shape[2]
    terms, pairs = right_blocks.shape[0], left_blocks.shape[0]
    slots, block = holders * cap, cap * rows
    entry_count = float(sectors * holders * width * width)
    couples = (pairs + min(pairs, sectors)) // 2

    packed = call(
        pack_kernel,
        [((vectors * block + 8, width), f32)] * holders,
        (main_memory(send_sector[0].T), main_memory(correction)),
        [hbm] * 2,
        [vmem] * holders,
        "pack",
        [
            pltpu.SMEM((cap, holders), jnp.int32),
            pltpu.VMEM(correction.shape, f32),
            pltpu.SemaphoreType.DMA,
            pltpu.SemaphoreType.DMA,
        ],
    )
    order = ring_order(ops)
    received = [
        lax.ppermute(
            packed[mask],
            ("ops", "sec", "rep"),
            [
                (order[i - 1] * holders + e, order[i] * holders + (e ^ mask))
                for i in range(ops)
                for e in range(holders)
            ],
        )
        for mask in range(holders)
    ]
    near = [packed[0]] + [
        lax.ppermute(packed[mask], ("sec", "rep"), [(e, e ^ mask) for e in range(holders)])
        for mask in range(1, holders)
    ]
    (plan,) = call(
        functools.partial(plan_kernel, pairs, sectors, cap, terms),
        [((5 * couples,), jnp.int32)],
        ((pair_slot * terms + pair_term) * sectors + pair_dst,),
        [smem],
        [smem],
        "plan",
        [pltpu.SMEM((sectors,), jnp.int32)],
    )
    high, low, right_both, right_low = call(
        operator_kernel,
        [
            ((couples, width, 2 * width), bf16),
            ((couples, width, 2 * width), bf16),
            ((2 * width, terms * width), bf16),
            ((width, terms * width), bf16),
        ],
        (plan, main_memory(pair_live), main_memory(left_blocks), main_memory(right_blocks)),
        [smem] + [hbm] * 3,
        [vmem] * 4,
        "operators",
        [
            pltpu.SMEM((pairs,), jnp.int32),
            pltpu.VMEM(left_blocks.shape, f32),
            pltpu.VMEM(right_blocks.shape, f32),
        ]
        + [pltpu.SemaphoreType.DMA] * 3,
    )

    joined = call(
        functools.partial(join_kernel, holders, block),
        [((slots * rows + (0 if vector else 8), width), f32) for vector in range(vectors)],
        received + [right_low],
        [vmem] * holders + [anywhere],
        [vmem] * vectors,
        "join",
    )
    pieces = [[value] for value in joined]
    for step in range(2, ops):
        for vector in range(vectors):
            value = pieces[vector][-1]
            if vector == 2 and step == 3:
                value = follow(value, near[1:])
            pieces[vector].append(ring_step(value, ops))

    inverse = None
    for vector in range(vectors):
        arguments = [plan, high, low, right_both, right_low]
        arguments += near + sum(pieces[: vector + 1], [])
        arguments += [inverse] if vector else []
        out = [((sectors, rows, width), f32)] * ops + ([] if vector else [((8, width), f32)])
        parts = call(
            functools.partial(apply_kernel, vector, holders, ops, rows, entry_count),
            out,
            arguments,
            [smem] + [vmem] * (len(arguments) - 1),
            [vmem] * len(out),
            "apply",
            [
                pltpu.VMEM((slots, width, width), f32),
                pltpu.VMEM((slots * terms, width, 2 * width), bf16),
                pltpu.VMEM((sectors, width, width), f32),
            ],
            small,
        )
        if vector == 0:
            inverse = parts[ops]
        total = parts[1]
        for step in range(2, ops):
            total = parts[step] + ring_step(total, ops)
        ends = [parts[0], ring_step(total, ops)]
        scratch = [pltpu.VMEM((sectors, rows, width), f32), pltpu.SemaphoreType.DMA]
        if vector == 0:
            sigma_blocks, search_basis = call(
                part_and_basis_kernel,
                [(correction.shape, f32)] * 2,
                ends + [inverse, correction],
                [vmem] * 4,
                [hbm, vmem],
                "part",
                scratch,
                small,
            )
        else:
            (sigma_blocks,) = call(
                functools.partial(part_kernel, vector),
                [(correction.shape, f32)],
                ends + [main_memory(sigma_blocks)],
                [vmem] * 2 + [hbm],
                [hbm],
                "part",
                scratch,
                small,
                {2: 0},
            )
    return (search_basis, sigma_blocks)


def solution(mesh):
    placed = (
        P(None, ("groups", "sec", "rep"), "ops", None),
        P(("groups", "ops", "sec", "rep"), None, None),
        P(("groups", "ops"), None, None),
        P(("groups", "sec", "rep"), None, None),
        P(("groups", "ops", "sec", "rep")),
        P(("groups", "ops", "sec", "rep")),
        P(("groups", "ops", "sec", "rep")),
        P(("groups", "ops", "sec", "rep")),
    )
    return jax.shard_map(
        local,
        mesh=mesh,
        in_specs=placed,
        out_specs=(
            P(None, ("groups", "sec", "rep"), "ops", None),
            P(None, ("groups", "sec", "rep"), "ops", None),
        ),
        check_vma=False,
    )
```

```python
import functools

import jax
import jax.numpy as jnp
from jax import lax
from jax.experimental import pallas as pl
from jax.experimental.pallas import tpu as pltpu
from jax.sharding import PartitionSpec as P

epsilon = 1e-06
vmem = pl.BlockSpec(memory_space=pltpu.VMEM)
smem = pl.BlockSpec(memory_space=pltpu.SMEM)
hbm = pl.BlockSpec(memory_space=pltpu.HBM)
anywhere = pl.BlockSpec(memory_space=pl.ANY)
limit = pltpu.CompilerParams(vmem_limit_bytes=48 * 1024 * 1024)
pairs_of_three = ((0, 0), (0, 1), (0, 2), (1, 1), (1, 2), (2, 2))
f32, bf16 = jnp.float32, jnp.bfloat16
dot = functools.partial(jnp.dot, preferred_element_type=f32)


def ring_order(ops):
    return [0] + list(range(1, ops, 2)) + list(range(ops - 2, 0, -2))


def ring_step(value, ops, back=False):
    order = ring_order(ops)
    order = order[::-1] if back else order
    return lax.ppermute(value, "ops", [(order[i - 1], order[i]) for i in range(ops)])


def shard_before(place, ops, steps):
    at = jnp.where(place % 2 == 1, (place + 1) // 2, (ops - place // 2) % ops)
    at = (at - steps + ops) % ops
    return jnp.where(at == 0, 0, jnp.where(at <= ops // 2, 2 * at - 1, 2 * (ops - at)))


def holder_index():
    return lax.axis_index("sec") * lax.axis_size("rep") + lax.axis_index("rep")


def main_memory(value):
    return pltpu.with_memory_space_constraint(value, pltpu.HBM)


def follow(value, others):
    return lax.optimization_barrier((value,) + tuple(others))[0] if others else value


def split(value):
    high = value.astype(bf16)
    return high, (value - high.astype(f32)).astype(bf16)


def pack_kernel(table_in, correction_in, *refs):
    *outs, table_ref, correction_ref, table_sem, correction_sem = refs
    table_copy = pltpu.make_async_copy(table_in, table_ref, table_sem)
    correction_copy = pltpu.make_async_copy(correction_in, correction_ref, correction_sem)
    correction_copy.start()
    table_copy.start()
    table_copy.wait()
    correction_copy.wait()
    vectors, _, rows, width = correction_ref.shape
    cap = table_ref.shape[0]
    here = holder_index()
    for mask, out in enumerate(outs):
        for slot in range(cap):
            sector = table_ref[slot, here ^ mask]
            filled = (sector >= 0).astype(f32)
            sector = jnp.maximum(sector, 0)
            for vector in range(vectors):
                start = (vector * cap + slot) * rows
                out[start : start + rows, :] = correction_ref[vector, sector] * filled
    tiles = []
    for i, j in pairs_of_three:
        total = jnp.sum(correction_ref[i] * correction_ref[j], axis=(0, 1))[None, :]
        total = jnp.sum(total, axis=1, keepdims=True)
        tiles.append(jnp.broadcast_to(total, (1, width)))
    tiles.append(jnp.zeros((2, width), f32))
    gram = jnp.concatenate(tiles, axis=0)
    for out in outs:
        out[out.shape[0] - 8 :, :] = gram


def join_kernel(holders, block, *refs):
    received, outs = refs[:holders], refs[holders + 1 :]
    for index, out in enumerate(outs):
        for sender, part_ref in enumerate(received):
            out[sender * block : (sender + 1) * block, :] = part_ref[index * block : (index + 1) * block, :]
    outs[0][holders * block :, :] = sum(ref[ref.shape[0] - 8 :, :] for ref in received)


def plan_kernel(pairs, sectors, cap, terms, packed_ref, plan_ref, next_ref):
    width = 5
    couples = plan_ref.shape[0] // width
    base = holder_index() * cap
    for sector in range(sectors):
        next_ref[sector] = 0

    def count_step(pair, carry):
        target = packed_ref[pair] & (sectors - 1)
        next_ref[target] += 1
        return carry

    def clear_step(couple, carry):
        for entry in range(3):
            plan_ref[width * couple + entry] = 0
        plan_ref[width * couple + 3] = -1
        plan_ref[width * couple + 4] = -1
        return carry

    lax.fori_loop(0, pairs, count_step, 0, unroll=4)
    lax.fori_loop(0, couples, clear_step, 0, unroll=4)
    start = jnp.int32(0)
    for sector in range(sectors):
        count = next_ref[sector]
        next_ref[sector] = start
        start = start + ((count + 1) & -2)

    def place_step(pair, carry):
        packed = packed_ref[pair]
        target = packed & (sectors - 1)
        packed = packed >> (sectors.bit_length() - 1)
        at = next_ref[target]
        next_ref[target] = at + 1
        first, side = (at >> 1) * width, at & 1
        slot = (packed >> (terms.bit_length() - 1)) ^ base
        plan_ref[first + side] = slot * terms + (packed & (terms - 1))
        plan_ref[first + 2] = target
        plan_ref[first + 3 + side] = pair
        return carry

    lax.fori_loop(0, pairs, place_step, 0, unroll=4)


def operator_kernel(plan_ref, live_in, left_in, right_in, *refs):
    high_ref, low_ref, right_both_ref, right_low_ref, live_ref, left_ref, right_ref, live_sem, left_sem, right_sem = refs
    width, terms = left_ref.shape[1], right_ref.shape[0]
    right_copy = pltpu.make_async_copy(right_in, right_ref, right_sem)
    live_copy = pltpu.make_async_copy(live_in, live_ref, live_sem)
    left_copy = pltpu.make_async_copy(left_in, left_ref, left_sem)
    right_copy.start()
    live_copy.start()
    left_copy.start()
    right_copy.wait()
    for term in range(terms):
        high, low = split(right_ref[term].T)
        columns = slice(term * width, (term + 1) * width)
        right_both_ref[:width, columns] = high
        right_both_ref[width:, columns] = high
        right_low_ref[:, columns] = low
    live_copy.wait()
    left_copy.wait()

    def couple_step(couple, carry):
        for side in range(2):
            pair = plan_ref[5 * couple + 3 + side]
            kept = jnp.where(pair >= 0, 1, 0)
            pair = jnp.maximum(pair, 0)
            scale = (live_ref[pair] * kept).astype(f32)
            high, low = split(left_ref[pair] * scale)
            high_ref[couple, :, side * width : (side + 1) * width] = high
            low_ref[couple, :, side * width : (side + 1) * width] = low
        return carry

    lax.fori_loop(0, high_ref.shape[0], couple_step, 0, unroll=4)


def inverse_rows(gram, entry_count):
    row = [gram[i : i + 1, :] / entry_count for i in range(6)]
    u_zero = jnp.sqrt(row[0] + epsilon)
    u_one = row[1] / u_zero
    u_two = row[2] / u_zero
    u_four = jnp.sqrt(row[3] + epsilon - u_one * u_one)
    u_five = (row[4] - u_one * u_two) / u_four
    u_eight = jnp.sqrt(row[5] + epsilon - u_two * u_two - u_five * u_five)
    v_zero = 1.0 / u_zero
    v_four = 1.0 / u_four
    v_eight = 1.0 / u_eight
    v_one = -u_one * v_zero * v_four
    v_five = -u_five * v_four * v_eight
    v_two = -(u_one * v_five + u_two * v_eight) * v_zero
    return [v_zero, v_one, v_two, v_four, v_five, v_eight]


def apply_kernel(vector, holders, ops, rows, entry_count, *refs):
    refs = list(refs)
    take = lambda count: [refs.pop(0) for _ in range(count)]
    plan_ref, high_ref, low_ref, right_both_ref, right_low_ref = take(5)
    near = take(holders)
    pieces = [take(ops - 1) for _ in range(vector + 1)]
    inverse_in = take(1)[0] if vector else None
    outs = take(ops)
    inverse_out = None if vector else take(1)[0]
    source_ref, chosen_ref, total_ref = refs
    place = lax.axis_index("ops")
    slots, width, _ = source_ref.shape
    terms = right_low_ref.shape[1] // width
    count = slots * rows
    if vector:
        inverse = inverse_in[...]
    else:
        gram = sum(ref[ref.shape[0] - 8 :, :] for ref in near + pieces[0])
        inverse = jnp.concatenate(inverse_rows(gram, entry_count) + [gram[6:]], axis=0)
        inverse_out[...] = inverse
    factors = [inverse[i : i + 1, :] for i, (_, column) in enumerate(pairs_of_three) if column == vector]
    cap = slots // holders
    block = cap * rows
    start = pl.multiple_of(place * rows, rows)
    for sender, ref in enumerate(near):
        value = sum(ref[j * block : (j + 1) * block, :] * factor for j, factor in enumerate(factors))
        source_ref[sender * cap : (sender + 1) * cap, pl.ds(start, rows), :] = value.reshape(cap, rows, width)
    for steps in range(1, ops):
        value = sum(pieces[j][steps - 1][:count, :] * factor for j, factor in enumerate(factors))
        start = pl.multiple_of(shard_before(place, ops, steps) * rows, rows)
        source_ref[:, pl.ds(start, rows), :] = value.reshape(slots, rows, width)

    def right_step(slot, carry):
        high, low = split(source_ref[slot])
        product = dot(jnp.concatenate([high, low], axis=1), right_both_ref[...])
        product += dot(high, right_low_ref[...])
        for term in range(terms):
            high, low = split(product[:, term * width : (term + 1) * width])
            chosen_ref[slot * terms + term, :, :width] = high
            chosen_ref[slot * terms + term, :, width:] = low
        return carry

    lax.fori_loop(0, slots, right_step, 0, unroll=8)
    total_ref[...] = jnp.zeros_like(total_ref)

    def couple_step(couple, carry):
        first, second = plan_ref[5 * couple], plan_ref[5 * couple + 1]
        chosen = jnp.concatenate([chosen_ref[first], chosen_ref[second]], axis=0)
        both = dot(high_ref[couple], chosen)
        rest = dot(low_ref[couple], chosen[:, :width])
        total_ref[plan_ref[5 * couple + 2]] += both[:, :width] + both[:, width:] + rest
        return carry

    lax.fori_loop(0, high_ref.shape[0], couple_step, 0, unroll=True)
    for steps in range(ops):
        start = pl.multiple_of(shard_before(place, ops, steps) * rows, rows)
        outs[steps][...] = total_ref[:, pl.ds(start, rows), :]


def part_kernel(vector, *refs):
    *terms, _, out, sum_ref, sum_sem = refs
    sum_ref[...] = sum(ref[...] for ref in terms)
    copy = pltpu.make_async_copy(sum_ref, out.at[vector], sum_sem)
    copy.start()
    copy.wait()


def part_and_basis_kernel(*refs):
    *terms, inverse_ref, correction_ref, out, basis_ref, sum_ref, sum_sem = refs
    sum_ref[...] = sum(ref[...] for ref in terms)
    copy = pltpu.make_async_copy(sum_ref, out.at[0], sum_sem)
    copy.start()
    inverse = inverse_ref[...]
    for k in range(basis_ref.shape[0]):
        picked = [(i, j) for i, (j, column) in enumerate(pairs_of_three) if column == k]
        basis_ref[k] = sum(correction_ref[j] * inverse[i : i + 1, :] for i, j in picked)
    copy.wait()


small = pl.CostEstimate(flops=1, bytes_accessed=1, transcendentals=0)


def call(kernel, out, inputs, specs, out_specs, name, scratch=(), cost=None, aliases={}):
    return pl.pallas_call(
        kernel,
        out_shape=[jax.ShapeDtypeStruct(shape, dtype) for shape, dtype in out],
        in_specs=specs,
        out_specs=out_specs,
        scratch_shapes=list(scratch),
        compiler_params=limit,
        cost_estimate=cost,
        input_output_aliases=aliases,
        name=name,
    )(*inputs)


def local(
    correction, left_blocks, right_blocks, send_sector, pair_slot, pair_term, pair_dst, pair_live
):
    ops, holders = lax.axis_size("ops"), lax.axis_size(("sec", "rep"))
    vectors, sectors, rows, width = correction.shape
    cap = send_sector.shape[2]
    terms, pairs = right_blocks.shape[0], left_blocks.shape[0]
    slots, block = holders * cap, cap * rows
    entry_count = float(sectors * holders * width * width)
    couples = (pairs + min(pairs, sectors)) // 2

    packed = call(
        pack_kernel,
        [((vectors * block + 8, width), f32)] * holders,
        (main_memory(send_sector[0].T), main_memory(correction)),
        [hbm] * 2,
        [vmem] * holders,
        "pack",
        [
            pltpu.SMEM((cap, holders), jnp.int32),
            pltpu.VMEM(correction.shape, f32),
            pltpu.SemaphoreType.DMA,
            pltpu.SemaphoreType.DMA,
        ],
    )
    order = ring_order(ops)
    received = [
        lax.ppermute(
            packed[mask],
            ("ops", "sec", "rep"),
            [
                (order[i - 1] * holders + e, order[i] * holders + (e ^ mask))
                for i in range(ops)
                for e in range(holders)
            ],
        )
        for mask in range(holders)
    ]
    near = [packed[0]] + [
        lax.ppermute(packed[mask], ("sec", "rep"), [(e, e ^ mask) for e in range(holders)])
        for mask in range(1, holders)
    ]
    (plan,) = call(
        functools.partial(plan_kernel, pairs, sectors, cap, terms),
        [((5 * couples,), jnp.int32)],
        ((pair_slot * terms + pair_term) * sectors + pair_dst,),
        [smem],
        [smem],
        "plan",
        [pltpu.SMEM((sectors,), jnp.int32)],
    )
    high, low, right_both, right_low = call(
        operator_kernel,
        [
            ((couples, width, 2 * width), bf16),
            ((couples, width, 2 * width), bf16),
            ((2 * width, terms * width), bf16),
            ((width, terms * width), bf16),
        ],
        (plan, main_memory(pair_live), main_memory(left_blocks), main_memory(right_blocks)),
        [smem] + [hbm] * 3,
        [vmem] * 4,
        "operators",
        [
            pltpu.SMEM((pairs,), jnp.int32),
            pltpu.VMEM(left_blocks.shape, f32),
            pltpu.VMEM(right_blocks.shape, f32),
        ]
        + [pltpu.SemaphoreType.DMA] * 3,
    )

    joined = call(
        functools.partial(join_kernel, holders, block),
        [((slots * rows + (0 if vector else 8), width), f32) for vector in range(vectors)],
        received + [right_low],
        [vmem] * holders + [anywhere],
        [vmem] * vectors,
        "join",
    )
    pieces = [[value] for value in joined]
    for step in range(2, ops):
        for vector in range(vectors):
            value = pieces[vector][-1]
            if vector == 2 and step == 3:
                value = follow(value, near[1:])
            pieces[vector].append(ring_step(value, ops))

    inverse = None
    for vector in range(vectors):
        arguments = [plan, high, low, right_both, right_low]
        arguments += near + sum(pieces[: vector + 1], [])
        arguments += [inverse] if vector else []
        out = [((sectors, rows, width), f32)] * ops + ([] if vector else [((8, width), f32)])
        parts = call(
            functools.partial(apply_kernel, vector, holders, ops, rows, entry_count),
            out,
            arguments,
            [smem] + [vmem] * (len(arguments) - 1),
            [vmem] * len(out),
            "apply",
            [
                pltpu.VMEM((slots, width, width), f32),
                pltpu.VMEM((slots * terms, width, 2 * width), bf16),
                pltpu.VMEM((sectors, width, width), f32),
            ],
            small,
        )
        if vector == 0:
            inverse = parts[ops]
        ends = [parts[0]]
        ahead = ops // 2
        total = parts[ahead]
        for step in range(ahead + 1, ops):
            total = parts[step] + ring_step(total, ops)
        ends.append(ring_step(total, ops))
        total = parts[ahead - 1]
        for step in range(ahead - 2, 0, -1):
            total = parts[step] + ring_step(total, ops, True)
        ends.append(ring_step(total, ops, True))
        scratch = [pltpu.VMEM((sectors, rows, width), f32), pltpu.SemaphoreType.DMA]
        if vector == 0:
            sigma_blocks, search_basis = call(
                part_and_basis_kernel,
                [(correction.shape, f32)] * 2,
                ends + [inverse, correction],
                [vmem] * (len(ends) + 2),
                [hbm, vmem],
                "part",
                scratch,
                small,
            )
        else:
            (sigma_blocks,) = call(
                functools.partial(part_kernel, vector),
                [(correction.shape, f32)],
                ends + [main_memory(sigma_blocks)],
                [vmem] * len(ends) + [hbm],
                [hbm],
                "part",
                scratch,
                small,
                {len(ends): 0},
            )
    return (search_basis, sigma_blocks)


def solution(mesh):
    placed = (
        P(None, ("groups", "sec", "rep"), "ops", None),
        P(("groups", "ops", "sec", "rep"), None, None),
        P(("groups", "ops"), None, None),
        P(("groups", "sec", "rep"), None, None),
        P(("groups", "ops", "sec", "rep")),
        P(("groups", "ops", "sec", "rep")),
        P(("groups", "ops", "sec", "rep")),
        P(("groups", "ops", "sec", "rep")),
    )
    return jax.shard_map(
        local,
        mesh=mesh,
        in_specs=placed,
        out_specs=(
            P(None, ("groups", "sec", "rep"), "ops", None),
            P(None, ("groups", "sec", "rep"), "ops", None),
        ),
        check_vma=False,
    )
```

```python
import functools

import jax
import jax.numpy as jnp
from jax import lax
from jax.experimental import pallas as pl
from jax.experimental.pallas import tpu as pltpu
from jax.sharding import PartitionSpec as P

epsilon = 1e-06
vmem = pl.BlockSpec(memory_space=pltpu.VMEM)
smem = pl.BlockSpec(memory_space=pltpu.SMEM)
hbm = pl.BlockSpec(memory_space=pltpu.HBM)
anywhere = pl.BlockSpec(memory_space=pl.ANY)
limit = pltpu.CompilerParams(vmem_limit_bytes=48 * 1024 * 1024)
pairs_of_three = ((0, 0), (0, 1), (0, 2), (1, 1), (1, 2), (2, 2))
f32, bf16 = jnp.float32, jnp.bfloat16
dot = functools.partial(jnp.dot, preferred_element_type=f32)


def ring_order(ops):
    return [0] + list(range(1, ops, 2)) + list(range(ops - 2, 0, -2))


def ring_step(value, ops, back=False):
    order = ring_order(ops)
    order = order[::-1] if back else order
    return lax.ppermute(value, "ops", [(order[i - 1], order[i]) for i in range(ops)])


def shard_before(place, ops, steps):
    at = jnp.where(place % 2 == 1, (place + 1) // 2, (ops - place // 2) % ops)
    at = (at - steps + ops) % ops
    return jnp.where(at == 0, 0, jnp.where(at <= ops // 2, 2 * at - 1, 2 * (ops - at)))


def holder_index():
    return lax.axis_index("sec") * lax.axis_size("rep") + lax.axis_index("rep")


def main_memory(value):
    return pltpu.with_memory_space_constraint(value, pltpu.HBM)


def follow(value, others):
    return lax.optimization_barrier((value,) + tuple(others))[0] if others else value


def split(value):
    high = value.astype(bf16)
    return high, (value - high.astype(f32)).astype(bf16)


def pack_kernel(table_in, correction_in, *refs):
    *outs, table_ref, correction_ref, table_sem, correction_sem = refs
    table_copy = pltpu.make_async_copy(table_in, table_ref, table_sem)
    correction_copy = pltpu.make_async_copy(correction_in, correction_ref, correction_sem)
    correction_copy.start()
    table_copy.start()
    table_copy.wait()
    correction_copy.wait()
    vectors, _, rows, width = correction_ref.shape
    cap = table_ref.shape[0]
    here = holder_index()
    for mask, out in enumerate(outs):
        for slot in range(cap):
            sector = table_ref[slot, here ^ mask]
            filled = (sector >= 0).astype(f32)
            sector = jnp.maximum(sector, 0)
            for vector in range(vectors):
                start = (vector * cap + slot) * rows
                out[start : start + rows, :] = correction_ref[vector, sector] * filled
    tiles = []
    for i, j in pairs_of_three:
        total = jnp.sum(correction_ref[i] * correction_ref[j], axis=(0, 1))[None, :]
        total = jnp.sum(total, axis=1, keepdims=True)
        tiles.append(jnp.broadcast_to(total, (1, width)))
    tiles.append(jnp.zeros((2, width), f32))
    gram = jnp.concatenate(tiles, axis=0)
    for out in outs:
        out[out.shape[0] - 8 :, :] = gram


def join_kernel(holders, block, *refs):
    both, outs = refs[: 2 * holders], refs[2 * holders + 1 :]
    vectors = len(outs) // 2
    for side in range(2):
        received, mine = both[side * holders : (side + 1) * holders], outs[side * vectors : (side + 1) * vectors]
        for index, out in enumerate(mine):
            for sender, part_ref in enumerate(received):
                out[sender * block : (sender + 1) * block, :] = part_ref[index * block : (index + 1) * block, :]
        mine[0][holders * block :, :] = sum(ref[ref.shape[0] - 8 :, :] for ref in received)


def plan_kernel(pairs, sectors, cap, terms, packed_ref, plan_ref, next_ref):
    width = 5
    couples = plan_ref.shape[0] // width
    base = holder_index() * cap
    for sector in range(sectors):
        next_ref[sector] = 0

    def count_step(pair, carry):
        target = packed_ref[pair] & (sectors - 1)
        next_ref[target] += 1
        return carry

    def clear_step(couple, carry):
        for entry in range(3):
            plan_ref[width * couple + entry] = 0
        plan_ref[width * couple + 3] = -1
        plan_ref[width * couple + 4] = -1
        return carry

    lax.fori_loop(0, pairs, count_step, 0, unroll=4)
    lax.fori_loop(0, couples, clear_step, 0, unroll=4)
    start = jnp.int32(0)
    for sector in range(sectors):
        count = next_ref[sector]
        next_ref[sector] = start
        start = start + ((count + 1) & -2)

    def place_step(pair, carry):
        packed = packed_ref[pair]
        target = packed & (sectors - 1)
        packed = packed >> (sectors.bit_length() - 1)
        at = next_ref[target]
        next_ref[target] = at + 1
        first, side = (at >> 1) * width, at & 1
        slot = (packed >> (terms.bit_length() - 1)) ^ base
        plan_ref[first + side] = slot * terms + (packed & (terms - 1))
        plan_ref[first + 2] = target
        plan_ref[first + 3 + side] = pair
        return carry

    lax.fori_loop(0, pairs, place_step, 0, unroll=4)


def operator_kernel(plan_ref, live_in, left_in, right_in, *refs):
    high_ref, low_ref, right_both_ref, right_low_ref, live_ref, left_ref, right_ref, live_sem, left_sem, right_sem = refs
    width, terms = left_ref.shape[1], right_ref.shape[0]
    right_copy = pltpu.make_async_copy(right_in, right_ref, right_sem)
    live_copy = pltpu.make_async_copy(live_in, live_ref, live_sem)
    left_copy = pltpu.make_async_copy(left_in, left_ref, left_sem)
    right_copy.start()
    live_copy.start()
    left_copy.start()
    right_copy.wait()
    for term in range(terms):
        high, low = split(right_ref[term].T)
        columns = slice(term * width, (term + 1) * width)
        right_both_ref[:width, columns] = high
        right_both_ref[width:, columns] = high
        right_low_ref[:, columns] = low
    live_copy.wait()
    left_copy.wait()

    def couple_step(couple, carry):
        for side in range(2):
            pair = plan_ref[5 * couple + 3 + side]
            kept = jnp.where(pair >= 0, 1, 0)
            pair = jnp.maximum(pair, 0)
            scale = (live_ref[pair] * kept).astype(f32)
            high, low = split(left_ref[pair] * scale)
            high_ref[couple, :, side * width : (side + 1) * width] = high
            low_ref[couple, :, side * width : (side + 1) * width] = low
        return carry

    lax.fori_loop(0, high_ref.shape[0], couple_step, 0, unroll=4)


def inverse_rows(gram, entry_count):
    row = [gram[i : i + 1, :] / entry_count for i in range(6)]
    u_zero = jnp.sqrt(row[0] + epsilon)
    u_one = row[1] / u_zero
    u_two = row[2] / u_zero
    u_four = jnp.sqrt(row[3] + epsilon - u_one * u_one)
    u_five = (row[4] - u_one * u_two) / u_four
    u_eight = jnp.sqrt(row[5] + epsilon - u_two * u_two - u_five * u_five)
    v_zero = 1.0 / u_zero
    v_four = 1.0 / u_four
    v_eight = 1.0 / u_eight
    v_one = -u_one * v_zero * v_four
    v_five = -u_five * v_four * v_eight
    v_two = -(u_one * v_five + u_two * v_eight) * v_zero
    return [v_zero, v_one, v_two, v_four, v_five, v_eight]


def apply_kernel(vector, holders, ops, rows, entry_count, *refs):
    refs = list(refs)
    take = lambda count: [refs.pop(0) for _ in range(count)]
    plan_ref, high_ref, low_ref, right_both_ref, right_low_ref = take(5)
    near = take(holders)
    pieces = [take(ops - 1) for _ in range(vector + 1)]
    inverse_in = take(1)[0] if vector else None
    outs = take(ops)
    inverse_out = None if vector else take(1)[0]
    source_ref, chosen_ref, total_ref = refs
    place = lax.axis_index("ops")
    slots, width, _ = source_ref.shape
    terms = right_low_ref.shape[1] // width
    count = slots * rows
    if vector:
        inverse = inverse_in[...]
    else:
        gram = sum(ref[ref.shape[0] - 8 :, :] for ref in near + pieces[0])
        inverse = jnp.concatenate(inverse_rows(gram, entry_count) + [gram[6:]], axis=0)
        inverse_out[...] = inverse
    factors = [inverse[i : i + 1, :] for i, (_, column) in enumerate(pairs_of_three) if column == vector]
    cap = slots // holders
    block = cap * rows
    start = pl.multiple_of(place * rows, rows)
    for sender, ref in enumerate(near):
        value = sum(ref[j * block : (j + 1) * block, :] * factor for j, factor in enumerate(factors))
        source_ref[sender * cap : (sender + 1) * cap, pl.ds(start, rows), :] = value.reshape(cap, rows, width)
    for steps in range(1, ops):
        value = sum(pieces[j][steps - 1][:count, :] * factor for j, factor in enumerate(factors))
        start = pl.multiple_of(shard_before(place, ops, steps) * rows, rows)
        source_ref[:, pl.ds(start, rows), :] = value.reshape(slots, rows, width)

    def right_step(slot, carry):
        high, low = split(source_ref[slot])
        product = dot(jnp.concatenate([high, low], axis=1), right_both_ref[...])
        product += dot(high, right_low_ref[...])
        for term in range(terms):
            high, low = split(product[:, term * width : (term + 1) * width])
            chosen_ref[slot * terms + term, :, :width] = high
            chosen_ref[slot * terms + term, :, width:] = low
        return carry

    lax.fori_loop(0, slots, right_step, 0, unroll=8)
    total_ref[...] = jnp.zeros_like(total_ref)

    def couple_step(couple, carry):
        first, second = plan_ref[5 * couple], plan_ref[5 * couple + 1]
        chosen = jnp.concatenate([chosen_ref[first], chosen_ref[second]], axis=0)
        both = dot(high_ref[couple], chosen)
        rest = dot(low_ref[couple], chosen[:, :width])
        total_ref[plan_ref[5 * couple + 2]] += both[:, :width] + both[:, width:] + rest
        return carry

    lax.fori_loop(0, high_ref.shape[0], couple_step, 0, unroll=True)
    for steps in range(ops):
        start = pl.multiple_of(shard_before(place, ops, steps) * rows, rows)
        outs[steps][...] = total_ref[:, pl.ds(start, rows), :]


def part_kernel(vector, *refs):
    *terms, _, out, sum_ref, sum_sem = refs
    sum_ref[...] = sum(ref[...] for ref in terms)
    copy = pltpu.make_async_copy(sum_ref, out.at[vector], sum_sem)
    copy.start()
    copy.wait()


def part_and_basis_kernel(*refs):
    *terms, inverse_ref, correction_ref, out, basis_ref, sum_ref, sum_sem = refs
    sum_ref[...] = sum(ref[...] for ref in terms)
    copy = pltpu.make_async_copy(sum_ref, out.at[0], sum_sem)
    copy.start()
    inverse = inverse_ref[...]
    for k in range(basis_ref.shape[0]):
        picked = [(i, j) for i, (j, column) in enumerate(pairs_of_three) if column == k]
        basis_ref[k] = sum(correction_ref[j] * inverse[i : i + 1, :] for i, j in picked)
    copy.wait()


small = pl.CostEstimate(flops=1, bytes_accessed=1, transcendentals=0)


def call(kernel, out, inputs, specs, out_specs, name, scratch=(), cost=None, aliases={}):
    return pl.pallas_call(
        kernel,
        out_shape=[jax.ShapeDtypeStruct(shape, dtype) for shape, dtype in out],
        in_specs=specs,
        out_specs=out_specs,
        scratch_shapes=list(scratch),
        compiler_params=limit,
        cost_estimate=cost,
        input_output_aliases=aliases,
        name=name,
    )(*inputs)


def local(
    correction, left_blocks, right_blocks, send_sector, pair_slot, pair_term, pair_dst, pair_live
):
    ops, holders = lax.axis_size("ops"), lax.axis_size(("sec", "rep"))
    vectors, sectors, rows, width = correction.shape
    cap = send_sector.shape[2]
    terms, pairs = right_blocks.shape[0], left_blocks.shape[0]
    slots, block = holders * cap, cap * rows
    entry_count = float(sectors * holders * width * width)
    couples = (pairs + min(pairs, sectors)) // 2

    packed = call(
        pack_kernel,
        [((vectors * block + 8, width), f32)] * holders,
        (main_memory(send_sector[0].T), main_memory(correction)),
        [hbm] * 2,
        [vmem] * holders,
        "pack",
        [
            pltpu.SMEM((cap, holders), jnp.int32),
            pltpu.VMEM(correction.shape, f32),
            pltpu.SemaphoreType.DMA,
            pltpu.SemaphoreType.DMA,
        ],
    )
    order = ring_order(ops)
    received = [
        lax.ppermute(
            packed[mask],
            ("ops", "sec", "rep"),
            [
                (order[i - 1] * holders + e, order[i] * holders + (e ^ mask))
                for i in range(ops)
                for e in range(holders)
            ],
        )
        for mask in range(holders)
    ]
    near = [packed[0]] + [
        lax.ppermute(packed[mask], ("sec", "rep"), [(e, e ^ mask) for e in range(holders)])
        for mask in range(1, holders)
    ]
    (plan,) = call(
        functools.partial(plan_kernel, pairs, sectors, cap, terms),
        [((5 * couples,), jnp.int32)],
        ((pair_slot * terms + pair_term) * sectors + pair_dst,),
        [smem],
        [smem],
        "plan",
        [pltpu.SMEM((sectors,), jnp.int32)],
    )
    high, low, right_both, right_low = call(
        operator_kernel,
        [
            ((couples, width, 2 * width), bf16),
            ((couples, width, 2 * width), bf16),
            ((2 * width, terms * width), bf16),
            ((width, terms * width), bf16),
        ],
        (plan, main_memory(pair_live), main_memory(left_blocks), main_memory(right_blocks)),
        [smem] + [hbm] * 3,
        [vmem] * 4,
        "operators",
        [
            pltpu.SMEM((pairs,), jnp.int32),
            pltpu.VMEM(left_blocks.shape, f32),
            pltpu.VMEM(right_blocks.shape, f32),
        ]
        + [pltpu.SemaphoreType.DMA] * 3,
    )

    def join(parts, after):
        return call(
            functools.partial(join_kernel, holders, block),
            [((slots * rows + (0 if vector else 8), width), f32) for vector in range(vectors)] * 2,
            list(parts) + [after],
            [vmem] * 2 * holders + [anywhere],
            [vmem] * 2 * vectors,
            "join",
        )

    ahead = ops // 2
    joined = join(received + near, right_low)
    joined, own = joined[:vectors], joined[vectors:]
    pieces = [[value] + [None] * (ops - 2) for value in joined]
    back = [[value] for value in own]
    for vector in range(vectors):
        for step in range(1, ops - ahead):
            value = back[vector][-1]
            if vector == 2:
                value = follow(value, [back[0][1]])
            back[vector].append(ring_step(value, ops, True))
            pieces[vector][ops - 1 - step] = back[vector][-1]
    for step in range(2, ahead + 1):
        for vector in range(vectors):
            value = pieces[vector][step - 2]
            others = [back[0][1]] if vector == 2 else []
            pieces[vector][step - 1] = ring_step(follow(value, others), ops)

    inverse = None
    for vector in range(vectors):
        arguments = [plan, high, low, right_both, right_low]
        arguments += near + sum(pieces[: vector + 1], [])
        arguments += [inverse] if vector else []
        out = [((sectors, rows, width), f32)] * ops + ([] if vector else [((8, width), f32)])
        parts = call(
            functools.partial(apply_kernel, vector, holders, ops, rows, entry_count),
            out,
            arguments,
            [smem] + [vmem] * (len(arguments) - 1),
            [vmem] * len(out),
            "apply",
            [
                pltpu.VMEM((slots, width, width), f32),
                pltpu.VMEM((slots * terms, width, 2 * width), bf16),
                pltpu.VMEM((sectors, width, width), f32),
            ],
            small,
        )
        if vector == 0:
            inverse = parts[ops]
        ends = [parts[0]]
        ahead = ops // 2
        total = parts[ahead]
        for step in range(ahead + 1, ops):
            total = parts[step] + ring_step(total, ops)
        ends.append(ring_step(total, ops))
        total = parts[ahead - 1]
        for step in range(ahead - 2, 0, -1):
            total = parts[step] + ring_step(total, ops, True)
        ends.append(ring_step(total, ops, True))
        scratch = [pltpu.VMEM((sectors, rows, width), f32), pltpu.SemaphoreType.DMA]
        if vector == 0:
            sigma_blocks, search_basis = call(
                part_and_basis_kernel,
                [(correction.shape, f32)] * 2,
                ends + [inverse, correction],
                [vmem] * (len(ends) + 2),
                [hbm, vmem],
                "part",
                scratch,
                small,
            )
        else:
            (sigma_blocks,) = call(
                functools.partial(part_kernel, vector),
                [(correction.shape, f32)],
                ends + [main_memory(sigma_blocks)],
                [vmem] * len(ends) + [hbm],
                [hbm],
                "part",
                scratch,
                small,
                {len(ends): 0},
            )
    return (search_basis, sigma_blocks)


def solution(mesh):
    placed = (
        P(None, ("groups", "sec", "rep"), "ops", None),
        P(("groups", "ops", "sec", "rep"), None, None),
        P(("groups", "ops"), None, None),
        P(("groups", "sec", "rep"), None, None),
        P(("groups", "ops", "sec", "rep")),
        P(("groups", "ops", "sec", "rep")),
        P(("groups", "ops", "sec", "rep")),
        P(("groups", "ops", "sec", "rep")),
    )
    return jax.shard_map(
        local,
        mesh=mesh,
        in_specs=placed,
        out_specs=(
            P(None, ("groups", "sec", "rep"), "ops", None),
            P(None, ("groups", "sec", "rep"), "ops", None),
        ),
        check_vma=False,
    )
```
